256 devices in a mesh: blk: 8 (over y_lo, x), grp: 32 (over z, y_hi, core).
Axes of the slice: x: 4, y: 4 (y_hi: 2, y_lo: 2; y = y_hi * 2 + y_lo), z: 8, core: 2. Of those that a mesh axis runs over, the one named last changes fastest.
Arguments:
- prefix: bfloat16 [8192, 4096], P('blk'), may hold values from -6 to 6
- latent: bfloat16 [2048, 4096], P(('blk', 'grp')), may hold values from -2.1 to 2.1
- limits: int32 [2048], P('blk'), may hold values from 1 to 8192, as said below
- gain_prefix: float32 [4096], replicated, may hold values from 0.1 to 1.9
- gain_latent: float32 [4096], replicated, may hold values from 0.1 to 1.9
- gain_state: float32 [4096], replicated, may hold values from 0.1 to 1.9
- cross_q: bfloat16 [4096, 4096], P('blk', 'grp'), may hold values from -4 to 4
- cross_k: bfloat16 [4096, 4096], P('blk', 'grp'), may hold values from -1 to 1
- cross_v: bfloat16 [4096, 4096], P('blk', 'grp'), may hold values from -0.09375 to 0.09375
- cross_o: bfloat16 [4096, 4096], P('grp', 'blk'), may hold values from -0.09375 to 0.09375
- delta_q: bfloat16 [4096, 4096], P('blk', 'grp'), may hold values from -0.046875 to 0.046875
- delta_k: bfloat16 [4096, 4096], P('blk', 'grp'), may hold values from -0.046875 to 0.046875
- delta_v: bfloat16 [4096, 4096], P('blk', 'grp'), may hold values from -0.046875 to 0.046875
- delta_o: bfloat16 [4096, 4096], P('grp', 'blk'), may hold values from -0.046875 to 0.046875
- self_q: bfloat16 [4096, 4096], P('blk', 'grp'), may hold values from -4 to 4
- self_k: bfloat16 [4096, 4096], P('blk', 'grp'), may hold values from -1 to 1
- self_v: bfloat16 [4096, 4096], P('blk', 'grp'), may hold values from -0.09375 to 0.09375
- self_o: bfloat16 [4096, 4096], P('grp', 'blk'), may hold values from -0.09375 to 0.09375
Outputs:
- latent_out: float32 [2048, 4096], P(('blk', 'grp'))
The draws below stay inside these ranges and needn't reach their ends.
Inputs may be any that keep to these rules, and one draw needn't show every extreme that they name: `limits`: the value of latent row i is at least i * 4 + 1; the last equals 8192.
All inputs are finite; a program needn't handle non-finite values.
Results may differ from the reference program's by a relative error of at most 0.019.
Values may be sent and summed in bfloat16 or wider, within the bound.
A program may use at most 128 MiB of HBM per device.

```python
import jax
import jax.numpy as jnp
from jax import lax

D = 4096
HEADS = 32
HD = 128
P_SIZE = 8192
L = 2048


def shared_base(key, salt):
    return jnp.clip(jax.random.normal(jax.random.fold_in(key, salt), (D, HEADS * HD), jnp.float32), -6.0, 6.0)


def query_matrix(key):
    own = jnp.clip(jax.random.normal(key, (D, HEADS * HD), jnp.float32), -6.0, 6.0) * (2.5 * D ** (-0.5))
    return jnp.clip(own, -4.0, 4.0).astype(jnp.bfloat16)


def draw_cross_k(key, part):
    base = shared_base(key, 101)
    return (base * D ** (-0.5)).astype(jnp.bfloat16)


def draw_cross_q(key, part):
    key = jax.random.fold_in(key, 2)
    return query_matrix(key)


def draw_self_k(key, part):
    base = shared_base(key, 102)
    return (base * D ** (-0.5)).astype(jnp.bfloat16)


def draw_self_q(key, part):
    key = jax.random.fold_in(key, 4)
    return query_matrix(key)


def draw_latent(key, part):
    key = jax.random.fold_in(key, 5)
    rows_drawn = jax.random.normal(key, (L, D), jnp.float32)
    return jnp.clip(0.35 * rows_drawn, -2.1, 2.1).astype(jnp.bfloat16)


def draw_limits(key, part):
    key = jax.random.fold_in(key, 6)
    frontier = jnp.arange(L, dtype=jnp.int32) * P_SIZE // L + 1
    picks = jax.random.randint(key, (L,), frontier, P_SIZE + 1, jnp.int32)
    return picks.at[L - 1].set(P_SIZE)


def shard_levels(key, dims, shards, smallest, largest):
    def one(axis_at, blocks):
        heights = jax.random.uniform(jax.random.fold_in(jax.random.fold_in(key, 6), axis_at), (blocks,), jnp.float32, smallest / len(shards), largest / len(shards))
        return jnp.repeat(jnp.exp(heights), dims[axis_at] // blocks).reshape((-1,) + (1,) * (len(dims) - axis_at - 1))

    loudness = one(*shards[0])
    for cut in shards[1:]:
        loudness = loudness * one(*cut)
    return loudness


def scatter_about(own_key, extent, scale, most, cuts=(), held_as=jnp.bfloat16):
    level = shard_levels(own_key, extent, cuts, -0.22, 0.18) if cuts else 1.0
    values = jax.random.normal(own_key, extent, jnp.float32) * scale * level
    return jnp.minimum(jnp.maximum(values, -most), most).astype(held_as)


def setup_inputs(seed: int = 0) -> dict:
    streams_of = jax.random.split(jax.random.key(seed), 19)
    return {
        "prefix": scatter_about(streams_of[0], (P_SIZE, D), 1.0, 6.0, ((0, 8),)),
        "latent": draw_latent(jax.random.fold_in(streams_of[18], 71), 0),
        "limits": draw_limits(jax.random.fold_in(streams_of[18], 71), 0),
        "gain_prefix": jnp.clip(1.0 + 0.18 * jax.random.normal(streams_of[3], (D,), jnp.float32), 0.1, 1.9),
        "gain_latent": jnp.clip(1.0 + 0.18 * jax.random.normal(streams_of[4], (D,), jnp.float32), 0.1, 1.9),
        "gain_state": jnp.clip(1.0 + 0.18 * jax.random.normal(streams_of[5], (D,), jnp.float32), 0.1, 1.9),
        "cross_q": draw_cross_q(jax.random.fold_in(streams_of[18], 71), 0),
        "cross_k": draw_cross_k(jax.random.fold_in(streams_of[18], 71), 0),
        "cross_v": scatter_about(streams_of[8], (D, HEADS * HD), D ** -0.5, 0.09375, ((0, 8), (1, 32))),
        "cross_o": scatter_about(streams_of[9], (HEADS * HD, D), (HEADS * HD) ** -0.5, 0.09375, ((0, 32), (1, 8))),
        "delta_q": scatter_about(streams_of[10], (D, HEADS * HD), (4 * D) ** -0.5, 0.046875, ((0, 8), (1, 32))),
        "delta_k": scatter_about(streams_of[11], (D, HEADS * HD), (4 * D) ** -0.5, 0.046875, ((0, 8), (1, 32))),
        "delta_v": scatter_about(streams_of[12], (D, HEADS * HD), (4 * D) ** -0.5, 0.046875, ((0, 8), (1, 32))),
        "delta_o": scatter_about(streams_of[13], (HEADS * HD, D), (4 * HEADS * HD) ** -0.5, 0.046875, ((0, 32), (1, 8))),
        "self_q": draw_self_q(jax.random.fold_in(streams_of[18], 71), 0),
        "self_k": draw_self_k(jax.random.fold_in(streams_of[18], 71), 0),
        "self_v": scatter_about(streams_of[16], (D, HEADS * HD), D ** -0.5, 0.09375, ((0, 8), (1, 32))),
        "self_o": scatter_about(streams_of[17], (HEADS * HD, D), (HEADS * HD) ** -0.5, 0.09375, ((0, 32), (1, 8))),
    }


epsilon = 1e-05

def rms_scale(rows_in, gain):
    values = rows_in.astype(jnp.float32)
    inverse = lax.rsqrt(lax.optimization_barrier(jnp.mean(values * values, axis=-1, keepdims=True)) + epsilon)
    return (values * inverse * gain.astype(jnp.float32)).astype(jnp.bfloat16)

def perturbed(weight, delta):
    return (weight.astype(jnp.float32) + delta.astype(jnp.float32)).astype(jnp.bfloat16)

def attend(queries, key_rows, value_rows, allowed):

    def split_heads(matrix):
        return jnp.transpose(matrix.reshape(matrix.shape[0], HEADS, HD), (1, 0, 2))

    def one_head(items):
        head_q, head_k, head_v = items
        scores = jnp.dot(head_q, head_k.T, preferred_element_type=jnp.float32) * HD ** (-0.5)
        scores = jnp.where(allowed, scores, -jnp.inf)
        row_max = lax.optimization_barrier(jnp.max(scores, axis=1, keepdims=True))
        exponent = jnp.where(allowed, jnp.exp(scores - row_max), 0.0)
        row_total = lax.optimization_barrier(jnp.sum(exponent, axis=1, keepdims=True))
        blended = jnp.dot(exponent, head_v.astype(jnp.float32), precision=lax.Precision.HIGHEST, preferred_element_type=jnp.float32)
        return (blended / row_total).astype(jnp.bfloat16)
    heads_out = lax.map(one_head, (split_heads(queries), split_heads(key_rows), split_heads(value_rows)))
    return jnp.transpose(heads_out, (1, 0, 2)).reshape(queries.shape[0], HEADS * HD)

def reference(prefix, latent, limits, gain_prefix, gain_latent, gain_state, cross_q, cross_k, cross_v, cross_o, delta_q, delta_k, delta_v, delta_o, self_q, self_k, self_v, self_o):
    w_query = perturbed(cross_q, delta_q)
    w_key = perturbed(cross_k, delta_k)
    w_value = perturbed(cross_v, delta_v)
    w_out = perturbed(cross_o, delta_o)
    prefix_n = rms_scale(prefix, gain_prefix)
    latent_n = rms_scale(latent, gain_latent)
    queries = jnp.dot(latent_n, w_query, preferred_element_type=jnp.float32).astype(jnp.bfloat16)
    key_rows = jnp.concatenate([jnp.dot(prefix_n, w_key, preferred_element_type=jnp.float32), jnp.dot(latent_n, w_key, preferred_element_type=jnp.float32)], axis=0).astype(jnp.bfloat16)
    value_rows = jnp.concatenate([jnp.dot(prefix_n, w_value, preferred_element_type=jnp.float32), jnp.dot(latent_n, w_value, preferred_element_type=jnp.float32)], axis=0).astype(jnp.bfloat16)
    latent_ids = jnp.arange(L, dtype=jnp.int32)
    prefix_ids = jnp.arange(P_SIZE, dtype=jnp.int32)
    self_allowed = latent_ids[None, :] <= latent_ids[:, None]
    allowed = jnp.concatenate([prefix_ids[None, :] < limits.astype(jnp.int32)[:, None], self_allowed], axis=1)
    mixed_cross = attend(queries, key_rows, value_rows, allowed)
    cross_sum = jnp.dot(mixed_cross, w_out, preferred_element_type=jnp.float32)
    carried = latent.astype(jnp.float32) + cross_sum
    carried_n = rms_scale(carried, gain_state)
    self_queries = jnp.dot(carried_n, self_q, preferred_element_type=jnp.float32).astype(jnp.bfloat16)
    self_keys = jnp.dot(carried_n, self_k, preferred_element_type=jnp.float32).astype(jnp.bfloat16)
    self_values = jnp.dot(carried_n, self_v, preferred_element_type=jnp.float32).astype(jnp.bfloat16)
    mixed_self = attend(self_queries, self_keys, self_values, self_allowed)
    return carried + jnp.dot(mixed_self, self_o, preferred_element_type=jnp.float32)
```

```python
import functools

import jax
import jax.numpy as jnp
from jax import lax
from jax.experimental import pallas as pl
from jax.experimental.pallas import tpu as pltpu
from jax.sharding import PartitionSpec as P

D = 4096
HD = 128
HALF = D // 2
EPS = 1e-05
SCALE = HD ** (-0.5)
LOW = -1e30
CLIP = -1e20
MESH = pl.DeviceIdType.MESH
F32 = jnp.float32
BF16 = jnp.bfloat16

N_SEM = 0


def _places(count):
    global N_SEM
    first = N_SEM
    N_SEM += count
    return first


S_WQ = _places(8)
S_WKV = _places(8)
S_WO = _places(8)
S_SQKV = _places(8)
S_SO = _places(8)
S_LIM = _places(8)
S_Q = _places(8)
S_O = _places(8)
S_ST = _places(8)
S_K2 = _places(8)
S_V2 = _places(8)
S_AGY = _places(2)
S_AGZ = _places(2 * 2 * 5)
S_AGC = _places(2 * 8)
S_RSC = _places(2)
S_RSZ = _places(2 * 2 * 2 * 5)
S_RSY = _places(2)


def rms_rows(values, gain):
    inverse = lax.rsqrt(jnp.sum(values * values, axis=1, keepdims=True) * (1.0 / D) + EPS)
    return values * inverse * gain


def pack_rows(rows):
    return jnp.concatenate([rows[:, :HALF], rows[:, HALF:]], axis=0)


def unpack_rows(packed):
    return jnp.concatenate([packed[:8], packed[8:]], axis=1)


def dot(a, b, ca=1, cb=0):
    return lax.dot_general(a, b, (((ca,), (cb,)), ((), ())), preferred_element_type=F32)


def layer_kernel(
    prefix, latent, limits, gain_p, gain_l, gain_s,
    cq, ck, cv, co, dq, dk, dv, do, sq, sk, sv, so_in,
    out,
    pre, wq, wkv, wo, sqkv, so, lim, qn, kn, vt, acc, qacc, scores,
    otx, orx, sttx, strx, mixed, k2, v2, o2,
    pk, pkr, gat, part, sib, rtx, rrx, ytx, yrx, carried,
    ss, rs, ls,
):
    b = lax.axis_index("blk")
    g = lax.axis_index("grp")
    x, yl = b % 4, b // 4
    z, yh, c = g // 4, (g // 2) % 2, g % 2

    def blk_to(i):
        return {"blk": ((yl + i // 4) % 2) * 4 + (x + i % 4) % 4, "grp": g}

    def blk_from(i):
        return ((yl + i // 4) % 2) * 4 + (x + 4 - i % 4) % 4

    def grp_at(zz, yy, cc):
        return {"blk": b, "grp": (zz * 2 + yy) * 2 + cc}

    sibling = grp_at(z, yh, 1 - c)
    across = grp_at(z, 1 - yh, c)
    above = grp_at((z + 1) % 8, yh, c)
    below = grp_at((z + 7) % 8, yh, c)
    vertical = (above, below)

    def remote(src, dst, place, device):
        return pltpu.make_async_remote_copy(
            src_ref=src, dst_ref=dst, send_sem=ss.at[place], recv_sem=rs.at[place],
            device_id=device, device_id_type=MESH,
        )

    sent = []

    def send(src, dst, place, device):
        copy = remote(src, dst, place, device)
        copy.start()
        sent.append(copy)

    def arrived(dst, place):
        remote(dst, dst, place, sibling).wait_recv()

    barrier = pltpu.get_barrier_semaphore()
    for i in range(1, 8):
        pl.semaphore_signal(barrier, inc=1, device_id=blk_to(i), device_id_type=MESH)
    for device in (sibling, across, above, below):
        pl.semaphore_signal(barrier, inc=1, device_id=device, device_id_type=MESH)

    loads = [
        pltpu.make_async_copy(prefix.at[pl.ds(t * 256, 256)], pre.at[pl.ds(t * 256, 256)], ls.at[t])
        for t in range(4)
    ]
    for load in loads:
        load.start()

    def perturbed(weight, delta):
        return (weight[...].astype(F32) + delta[...].astype(F32)).astype(BF16)

    rows_l = rms_rows(latent[...].astype(F32), gain_l[...])
    pk[0] = pack_rows(rows_l).astype(BF16)
    lim[0] = jnp.broadcast_to(limits[...], (8, 256))
    wq[0] = perturbed(cq, dq)
    wkv[0, :, :HD] = perturbed(ck, dk)
    wkv[0, :, HD:] = perturbed(cv, dv)
    pl.semaphore_wait(barrier, 11)

    def gather_begin(u):
        send(pk.at[u], pkr.at[u], S_AGY + u, across)

    def gather_pair(u, rows):
        arrived(pkr.at[u], S_AGY + u)
        other = unpack_rows(pkr[u].astype(F32))
        low = jnp.where(yh == 0, rows, other)
        high = jnp.where(yh == 0, other, rows)
        gat[u, z, c] = jnp.concatenate([low, high], axis=0).astype(BF16)
        own = gat.at[u, z, c]
        for way in range(2):
            send(own, own, S_AGZ + (u * 2 + way) * 5 + 1, vertical[way])
        send(own, own, S_AGC + u * 8, sibling)

    def gather_step(u, k):
        for way in range(2):
            zz = (z + 8 - k) % 8 if way == 0 else (z + k) % 8
            chunk = gat.at[u, zz, c]
            if k < 4:
                arrived(chunk, S_AGZ + (u * 2 + way) * 5 + k)
                onward = chunk
                if k == 3:
                    onward = gat.at[u, zz, c, :, pl.ds(way * HALF, HALF)]
                send(onward, onward, S_AGZ + (u * 2 + way) * 5 + k + 1, vertical[way])
                send(chunk, chunk, S_AGC + u * 8 + (k if way == 0 else 8 - k), sibling)
            else:
                piece = gat.at[u, zz, c, :, pl.ds(way * HALF, HALF)]
                arrived(piece, S_AGZ + (u * 2 + way) * 5 + 4)
        if k == 4:
            chunk = gat.at[u, (z + 4) % 8, c]
            send(chunk, chunk, S_AGC + u * 8 + 4, sibling)

    def gather_end(u):
        for k in range(8):
            arrived(gat.at[u, (z + 8 - k) % 8, 1 - c], S_AGC + u * 8 + k)

    gather_begin(0)
    for i in range(1, 8):
        send(lim.at[0], lim.at[i], S_LIM + i, blk_to(i))
    for i in range(1, 8):
        send(wq.at[0], wq.at[i], S_WQ + i, blk_to(i))
    for i in range(1, 8):
        send(wkv.at[0], wkv.at[i], S_WKV + i, blk_to(i))
    gather_pair(0, rows_l)

    def norm_prefix(t):
        loads[t].wait()

        def tile(n, carry):
            rows = pl.ds(pl.multiple_of(t * 256 + n * 16, 16), 16)
            pre[rows, :] = rms_rows(pre[rows, :].astype(F32), gain_p[...]).astype(BF16)
            return carry

        lax.fori_loop(0, 16, tile, 0)

    for t in range(4):
        norm_prefix(t)
        gather_step(0, t + 1)
    wo[0] = perturbed(co, do)
    sqkv[0, :, :HD] = sq[...]
    sqkv[0, :, HD:2 * HD] = sk[...]
    sqkv[0, :, 2 * HD:] = sv[...]
    so[0] = so_in[...]
    gather_end(0)

    def latent_slice(u, i):
        columns = pl.ds(pl.multiple_of(blk_from(i) * 512, 512), 512)
        return gat[u, :, :, :, columns].reshape(256, 512)

    def natural(values, width):
        cut = values.reshape(8, 2, 2, 8, width)
        swapped = jnp.concatenate(
            [cut[:, :, yy][:, :, None] for yy in range(2)], axis=2
        )
        order = jnp.stack([cut[:, cc, yy] for yy in range(2) for cc in range(2)], axis=1)
        del swapped
        return order.reshape(256, width)

    def query_part(i, carry):
        @pl.when(i > 0)
        def _():
            arrived(wq.at[i], S_WQ + i)

        part_q = dot(latent_slice(0, i), wq[i])

        @pl.when(i == 0)
        def _():
            qacc[:, :HD] = part_q

        @pl.when(i > 0)
        def _():
            qacc[:, :HD] = qacc[:, :HD] + part_q

        return carry

    lax.fori_loop(0, 8, query_part, 0)
    qn[0] = natural(qacc[:, :HD], HD).astype(BF16)
    for i in range(1, 8):
        send(qn.at[0], qn.at[i], S_Q + i, blk_to(i))
    for i in range(1, 8):
        send(wo.at[0], wo.at[i], S_WO + i, blk_to(i))

    def keyval_part(i, carry):
        @pl.when(i > 0)
        def _():
            arrived(wkv.at[i], S_WKV + i)

        columns = pl.ds(pl.multiple_of(blk_from(i) * 512, 512), 512)
        for t in range(5):
            rows = pl.ds(t * 256, 256)
            if t < 4:
                piece = dot(pre[rows, columns], wkv[i])
            else:
                piece = dot(latent_slice(0, i), wkv[i])

            @pl.when(i == 0)
            def _():
                acc[rows, :] = piece

            @pl.when(i > 0)
            def _():
                acc[rows, :] = acc[rows, :] + piece

        return carry

    lax.fori_loop(0, 8, keyval_part, 0)
    for t in range(5):
        rows = pl.ds(t * 256, 256)
        values = acc[rows, :]
        if t == 4:
            values = natural(values, 2 * HD)
        kn[rows, :] = values[:, :HD].astype(BF16)
        vt[:, rows] = values[:, HD:].T.astype(BF16)

    def attend(i, carry):
        @pl.when(i > 0)
        def _():
            arrived(qn.at[i], S_Q + i)
            arrived(lim.at[i], S_LIM + i)

        source = blk_from(i)
        queries = qn[i]
        seen = lim[i][0:1, :]
        high = jnp.full((8, 256), CLIP, F32)
        for t in range(5):
            s = dot(kn[pl.ds(t * 256, 256), :], queries, 1, 1) * SCALE
            ids = lax.broadcasted_iota(jnp.int32, (256, 256), 0)
            if t < 4:
                allowed = ids + (b * 1024 + t * 256) < seen
            else:
                allowed = ids + b * 256 <= lax.broadcasted_iota(jnp.int32, (256, 256), 1) + source * 256
            s = jnp.where(allowed, s, LOW)
            scores[pl.ds(t * 256, 256), :] = s
            high = jnp.maximum(high, jnp.max(s.reshape(32, 8, 256), axis=0))
        top = jnp.max(high, axis=0, keepdims=True)
        total = jnp.zeros((8, 256), F32)
        weighted = jnp.zeros((HD, 256), F32)
        for t in range(5):
            e = jnp.exp(scores[pl.ds(t * 256, 256), :] - top)
            total = total + jnp.sum(e.reshape(32, 8, 256), axis=0)
            weighted = weighted + dot(vt[:, pl.ds(t * 256, 256)], e.astype(BF16))
        total = jnp.sum(total, axis=0, keepdims=True)
        otx[i] = weighted.astype(BF16)
        first = lax.broadcasted_iota(jnp.int32, (8, 256), 0) == 0
        sttx[i] = jnp.where(first, top, total)

        @pl.when(i > 0)
        def _():
            back = {"blk": source, "grp": g}
            remote(otx.at[i], orx.at[i], S_O + i, back).start()
            remote(sttx.at[i], strx.at[i], S_ST + i, back).start()

        return carry

    lax.fori_loop(0, 8, attend, 0)
    for i in range(1, 8):
        back = {"blk": blk_from(i), "grp": g}
        sent.append(remote(otx.at[i], orx.at[i], S_O + i, back))
        sent.append(remote(sttx.at[i], strx.at[i], S_ST + i, back))
    for i in range(1, 8):
        send(sqkv.at[0], sqkv.at[i], S_SQKV + i, blk_to(i))

    orx[0] = otx[0]
    strx[0] = sttx[0]
    for i in range(1, 8):
        arrived(orx.at[i], S_O + i)
        arrived(strx.at[i], S_ST + i)
    tops = [strx[i][0:1, :] for i in range(8)]
    top = functools.reduce(jnp.maximum, tops)
    total = jnp.zeros((1, 256), F32)
    weighted = jnp.zeros((HD, 256), F32)
    for i in range(8):
        factor = jnp.exp(tops[i] - top)
        total = total + factor * strx[i][1:2, :]
        weighted = weighted + orx[i].astype(F32) * factor
    mixed[0] = (weighted / total).T.astype(BF16)

    def project_and_sum(u, weight, place):
        def columns_of(i, carry):
            @pl.when(i > 0)
            def _():
                arrived(weight.at[i], place + i)

            columns = pl.ds(pl.multiple_of(blk_from(i) * 512, 512), 512)
            y = dot(mixed[u], weight[i]).reshape(8, 2, 2, 8, 512)
            for cc in range(2):
                part[u, cc, :, :, columns] = y[:, :, cc].reshape(8, 16, 512).astype(BF16)
            return carry

        lax.fori_loop(0, 8, columns_of, 0)
        send(part.at[u, 1 - c], sib.at[u], S_RSC + u, sibling)
        arrived(sib.at[u], S_RSC + u)

        def chip_sum(zz, h):
            columns = pl.ds(h * HALF, HALF)
            return part[u, c, zz, :, columns].astype(F32) + sib[u, zz, :, columns].astype(F32)

        for k in (4, 3, 2, 1):
            for way, h in ((0, 0), (1, 1), (0, 1), (1, 0)):
                start = 4 if way == h else 3
                if k > start:
                    continue
                zz = (z + k) % 8 if way == 0 else (z + 8 - k) % 8
                value = chip_sum(zz, h)
                at = S_RSZ + ((u * 2 + way) * 2 + h) * 5
                if k < start:
                    arrived(rrx.at[u, way, h, k], at + k + 1)
                    value = value + rrx[u, way, h, k].astype(F32)
                rtx[u, way, h, k - 1] = value.astype(BF16)
                send(rtx.at[u, way, h, k - 1], rrx.at[u, way, h, k - 1], at + k, vertical[way])
        halves = []
        for h in range(2):
            value = chip_sum(z, h)
            for way in range(2):
                arrived(rrx.at[u, way, h, 0], S_RSZ + ((u * 2 + way) * 2 + h) * 5 + 1)
                value = value + rrx[u, way, h, 0].astype(F32)
            halves.append(value)
        both = jnp.concatenate(halves, axis=1)
        mine = jnp.where(yh == 0, both[:8], both[8:])
        ytx[u] = pack_rows(jnp.where(yh == 0, both[8:], both[:8])).astype(BF16)
        send(ytx.at[u], yrx.at[u], S_RSY + u, across)
        arrived(yrx.at[u], S_RSY + u)
        return mine + unpack_rows(yrx[u].astype(F32))

    carried[...] = latent[...].astype(F32) + project_and_sum(0, wo, S_WO)

    rows_c = rms_rows(carried[...], gain_s[...])
    pk[1] = pack_rows(rows_c).astype(BF16)
    gather_begin(1)
    gather_pair(1, rows_c)
    for k in range(1, 5):
        gather_step(1, k)
    gather_end(1)

    def self_part(i, carry):
        @pl.when(i > 0)
        def _():
            arrived(sqkv.at[i], S_SQKV + i)

        piece = dot(latent_slice(1, i), sqkv[i])

        @pl.when(i == 0)
        def _():
            qacc[...] = piece

        @pl.when(i > 0)
        def _():
            qacc[...] = qacc[...] + piece

        return carry

    lax.fori_loop(0, 8, self_part, 0)
    qkv = natural(qacc[...], 3 * HD)
    queries = qkv[:, :HD].astype(BF16)
    k2[0] = qkv[:, HD:2 * HD].astype(BF16)
    v2[0] = qkv[:, 2 * HD:].T.astype(BF16)

    def later(i):
        there = {"blk": jnp.minimum(b + i, 7), "grp": g}
        return (
            remote(k2.at[0], k2.at[i], S_K2 + i, there),
            remote(v2.at[0], v2.at[i], S_V2 + i, there),
        )

    for i in range(1, 8):
        @pl.when(b + i < 8)
        def _():
            for copy in later(i):
                copy.start()
    for i in range(1, 8):
        send(so.at[0], so.at[i], S_SO + i, blk_to(i))

    def absorb(s, values, top, total, weighted):
        new = jnp.maximum(top, jnp.max(s, axis=0, keepdims=True))
        e = jnp.exp(s - new)
        factor = jnp.exp(top - new)
        total = total * factor + jnp.sum(e, axis=0, keepdims=True)
        return new, total, weighted * factor + dot(values, e.astype(BF16))

    s = dot(k2[0], queries, 1, 1) * SCALE
    s = jnp.where(
        lax.broadcasted_iota(jnp.int32, (256, 256), 0) <= lax.broadcasted_iota(jnp.int32, (256, 256), 1),
        s, LOW,
    )
    state = absorb(
        s, v2[0], jnp.full((1, 256), CLIP, F32), jnp.zeros((1, 256), F32), jnp.zeros((HD, 256), F32)
    )

    def self_block(i, state):
        arrived(k2.at[i], S_K2 + i)
        arrived(v2.at[i], S_V2 + i)
        return absorb(dot(k2[i], queries, 1, 1) * SCALE, v2[i], *state)

    top, total, weighted = lax.fori_loop(1, b + 1, self_block, state)
    mixed[1] = (weighted / total).T.astype(BF16)

    out[...] = carried[...] + project_and_sum(1, so, S_SO)

    for i in range(1, 8):
        @pl.when(b + i < 8)
        def _():
            for copy in later(i):
                copy.wait_send()
    for copy in sent:
        copy.wait_send()


def shards(*arguments):
    prefix, latent, limits, gain_p, gain_l, gain_s, *weights = arguments
    vmem = pl.BlockSpec(memory_space=pltpu.VMEM)
    sem = pltpu.SemaphoreType.DMA
    scratch = [
        ((1024, D), BF16),
        ((8, 512, HD), BF16),
        ((8, 512, 2 * HD), BF16),
        ((8, HD, 512), BF16),
        ((8, 512, 3 * HD), BF16),
        ((8, HD, 512), BF16),
        ((8, 8, 256), jnp.int32),
        ((8, 256, HD), BF16),
        ((1280, HD), BF16),
        ((HD, 1280), BF16),
        ((1280, 2 * HD), F32),
        ((256, 3 * HD), F32),
        ((1280, 256), F32),
        ((8, HD, 256), BF16),
        ((8, HD, 256), BF16),
        ((8, 8, 256), F32),
        ((8, 8, 256), F32),
        ((2, 256, HD), BF16),
        ((8, 256, HD), BF16),
        ((8, HD, 256), BF16),
        ((HD, 256), F32),
        ((2, 16, HALF), BF16),
        ((2, 16, HALF), BF16),
        ((2, 8, 2, 16, D), BF16),
        ((2, 2, 8, 16, D), BF16),
        ((2, 8, 16, D), BF16),
        ((2, 2, 2, 4, 16, HALF), BF16),
        ((2, 2, 2, 4, 16, HALF), BF16),
        ((2, 16, HALF), BF16),
        ((2, 16, HALF), BF16),
        ((8, D), F32),
    ]
    return pl.pallas_call(
        layer_kernel,
        out_shape=jax.ShapeDtypeStruct((8, D), F32),
        in_specs=[pl.BlockSpec(memory_space=pl.ANY)] + [vmem] * 17,
        out_specs=vmem,
        scratch_shapes=[pltpu.VMEM(shape, dtype) for shape, dtype in scratch]
        + [sem((N_SEM,)), sem((N_SEM,)), sem((4,))],
        compiler_params=pltpu.CompilerParams(
            collective_id=0, has_side_effects=True, vmem_limit_bytes=56 * 1024 * 1024
        ),
        name="layer",
    )(
        prefix, latent, limits.reshape(1, -1),
        gain_p.reshape(1, -1), gain_l.reshape(1, -1), gain_s.reshape(1, -1), *weights,
    )


def solution(mesh):
    return jax.shard_map(
        shards,
        mesh=mesh,
        in_specs=(
            P("blk", None), P(("blk", "grp"), None), P("blk"), P(), P(), P(),
            P("blk", "grp"), P("blk", "grp"), P("blk", "grp"), P("grp", "blk"),
            P("blk", "grp"), P("blk", "grp"), P("blk", "grp"), P("grp", "blk"),
            P("blk", "grp"), P("blk", "grp"), P("blk", "grp"), P("grp", "blk"),
        ),
        out_specs=P(("blk", "grp"), None),
        check_vma=False,
    )
```

```python
import functools

import jax
import jax.numpy as jnp
from jax import lax
from jax.experimental import pallas as pl
from jax.experimental.pallas import tpu as pltpu
from jax.sharding import PartitionSpec as P

D = 4096
HD = 128
HALF = D // 2
EPS = 1e-05
SCALE = HD ** (-0.5)
LOW = -1e30
CLIP = -1e20
MESH = pl.DeviceIdType.MESH
F32 = jnp.float32
BF16 = jnp.bfloat16

N_SEM = 0


def _places(count):
    global N_SEM
    first = N_SEM
    N_SEM += count
    return first


S_WX = _places(10)
S_WY = _places(10)
S_WO = _places(10)
S_SQKV = _places(10)
S_SO = _places(10)
S_LIM = _places(8)
S_Q = _places(8)
S_O = _places(8)
S_ST = _places(8)
S_K2 = _places(8)
S_V2 = _places(8)
S_AGY = _places(2)
S_AGZ = _places(2 * 2 * 5)
S_AGC = _places(2 * 8)
S_RSC = _places(4)
S_RSZ = _places(2 * 2 * 2 * 5)
S_RSY = _places(2)


def rms_rows(values, gain):
    inverse = lax.rsqrt(jnp.sum(values * values, axis=1, keepdims=True) * (1.0 / D) + EPS)
    return values * inverse * gain


def pack_rows(rows):
    return jnp.concatenate([rows[:, :HALF], rows[:, HALF:]], axis=0)


def unpack_rows(packed):
    return jnp.concatenate([packed[:8], packed[8:]], axis=1)


def dot(a, b, ca=1, cb=0):
    return lax.dot_general(a, b, (((ca,), (cb,)), ((), ())), preferred_element_type=F32)


def layer_kernel(
    prefix, latent, limits, gain_p, gain_l, gain_s,
    cq, ck, cv, co, dq, dk, dv, do, sq, sk, sv, so_in,
    out,
    pre, wqkv, wo, sqkv, so, lim, qn, kn, vt, acc, qacc, scores,
    otx, orx, sttx, strx, mixed, k2, v2,
    pk, pkr, gat, part, sib, rtx, rrx, ytx, yrx, ztx, zrx,
    ss, rs, ls,
):
    b = lax.axis_index("blk")
    g = lax.axis_index("grp")
    x, yl = b % 4, b // 4
    z, yh, c = g // 4, (g // 2) % 2, g % 2

    def blk_to(i):
        return {"blk": ((yl + i // 4) % 2) * 4 + (x + i % 4) % 4, "grp": g}

    def blk_from(i):
        return ((yl + i // 4) % 2) * 4 + (x + 4 - i % 4) % 4

    def grp_at(zz, yy, cc):
        return {"blk": b, "grp": (zz * 2 + yy) * 2 + cc}

    sibling = grp_at(z, yh, 1 - c)
    across = grp_at(z, 1 - yh, c)
    above = grp_at((z + 1) % 8, yh, c)
    below = grp_at((z + 7) % 8, yh, c)
    vertical = (above, below)

    def remote(src, dst, place, device):
        return pltpu.make_async_remote_copy(
            src_ref=src, dst_ref=dst, send_sem=ss.at[place], recv_sem=rs.at[place],
            device_id=device, device_id_type=MESH,
        )

    sent = []

    def send(src, dst, place, device):
        copy = remote(src, dst, place, device)
        copy.start()
        sent.append(copy)

    def arrived(dst, place):
        remote(dst, dst, place, sibling).wait_recv()

    barrier = pltpu.get_barrier_semaphore()
    for i in range(1, 8):
        pl.semaphore_signal(barrier, inc=1, device_id=blk_to(i), device_id_type=MESH)
    for device in (sibling, across, above, below):
        pl.semaphore_signal(barrier, inc=1, device_id=device, device_id_type=MESH)

    loads = [
        pltpu.make_async_copy(prefix.at[pl.ds(t * 256, 256)], pre.at[pl.ds(t * 256, 256)], ls.at[t])
        for t in range(4)
    ]
    for load in loads:
        load.start()

    def perturbed(weight, delta):
        return (weight[...].astype(F32) + delta[...].astype(F32)).astype(BF16)

    rows_l = latent[...].astype(F32)
    pk[...] = pack_rows(rows_l).astype(BF16)
    lim[0] = jnp.broadcast_to(limits[...], (8, 256))
    wqkv[0, :, :HD] = perturbed(cq, dq)
    wqkv[0, :, HD:2 * HD] = perturbed(ck, dk)
    wqkv[0, :, 2 * HD:] = perturbed(cv, dv)
    pl.semaphore_wait(barrier, 11)

    right, left, beside = blk_to(1), blk_to(3), blk_to(4)

    def spread(buf, start, rows, place, y_first, stage):
        def cut(i, piece=None):
            if piece is None:
                return buf.at[i, pl.ds(start, rows)]
            return buf.at[i, pl.ds(start + piece * (rows // 2), rows // 2)]

        if stage == 0:
            send(cut(0), cut(4), place + 4, beside)
            send(cut(0), cut(1), place + 1, right)
            send(cut(0), cut(3), place + 3, left)
        elif y_first and stage == 1:
            arrived(cut(4), place + 4)
            send(cut(4), cut(5), place + 5, right)
            send(cut(4), cut(7), place + 7, left)
        elif y_first and stage == 2:
            arrived(cut(1), place + 1)
            send(cut(1, 0), cut(2, 0), place + 2, right)
            arrived(cut(3), place + 3)
            send(cut(3, 1), cut(2, 1), place + 8, left)
        elif y_first and stage == 3:
            arrived(cut(5), place + 5)
            send(cut(5, 0), cut(6, 0), place + 6, right)
            arrived(cut(7), place + 7)
            send(cut(7, 1), cut(6, 1), place + 9, left)
        elif y_first:
            arrived(cut(2, 0), place + 2)
            arrived(cut(2, 1), place + 8)
            arrived(cut(6, 0), place + 6)
            arrived(cut(6, 1), place + 9)
        elif stage == 1:
            arrived(cut(1), place + 1)
            send(cut(1, 0), cut(2, 0), place + 2, right)
            send(cut(1), cut(5), place + 5, beside)
            arrived(cut(3), place + 3)
            send(cut(3, 1), cut(2, 1), place + 8, left)
            send(cut(3), cut(7), place + 7, beside)
        elif stage == 2:
            arrived(cut(2, 0), place + 2)
            arrived(cut(2, 1), place + 8)
            send(cut(2), cut(6), place + 6, beside)
        elif stage == 3:
            arrived(cut(4), place + 4)
            arrived(cut(5), place + 5)
            arrived(cut(7), place + 7)
        else:
            arrived(cut(6), place + 6)

    def spread_cross(stage):
        spread(wqkv, 0, 256, S_WX, False, stage)
        spread(wqkv, 256, 256, S_WY, True, stage)

    def spread_self(stage):
        spread(sqkv, 0, 512, S_SQKV, True, stage)

    def spread_wo(stage):
        spread(wo, 0, HD, S_WO, True, stage)

    def spread_so(stage):
        spread(so, 0, HD, S_SO, True, stage)

    def own_and_other(own, other):
        return jnp.concatenate([jnp.where(yh == 0, own, other), jnp.where(yh == 0, other, own)], axis=0)

    def gather_begin(u, rows, gain):
        gat[u, z, c] = rms_rows(rows, gain).astype(BF16)
        own = gat.at[u, z, c]
        for way in range(2):
            send(own, own, S_AGZ + (u * 2 + way) * 5 + 1, vertical[way])
        send(own, own, S_AGC + u * 8, sibling)

    def gather_step(u, k):
        for way in range(2):
            zz = (z + 8 - k) % 8 if way == 0 else (z + k) % 8
            chunk = gat.at[u, zz, c]
            if k < 4:
                arrived(chunk, S_AGZ + (u * 2 + way) * 5 + k)
                onward = chunk
                if k == 3:
                    onward = gat.at[u, zz, c, :, pl.ds(way * HALF, HALF)]
                send(onward, onward, S_AGZ + (u * 2 + way) * 5 + k + 1, vertical[way])
                send(chunk, chunk, S_AGC + u * 8 + (k if way == 0 else 8 - k), sibling)
            else:
                piece = gat.at[u, zz, c, :, pl.ds(way * HALF, HALF)]
                arrived(piece, S_AGZ + (u * 2 + way) * 5 + 4)
        if k == 4:
            chunk = gat.at[u, (z + 4) % 8, c]
            send(chunk, chunk, S_AGC + u * 8 + 4, sibling)

    def gather_end(u):
        for k in range(8):
            arrived(gat.at[u, (z + 8 - k) % 8, 1 - c], S_AGC + u * 8 + k)

    send(pk, pkr, S_AGY, across)
    spread_cross(0)
    for i in range(1, 8):
        send(lim.at[0], lim.at[i], S_LIM + i, blk_to(i))

    def norm_prefix(t):
        loads[t].wait()

        def tile(n, carry):
            rows = pl.ds(pl.multiple_of(t * 256 + n * 16, 16), 16)
            pre[rows, :] = rms_rows(pre[rows, :].astype(F32), gain_p[...]).astype(BF16)
            return carry

        lax.fori_loop(0, 16, tile, 0)

    def prefix_part(i):
        columns = pl.ds(pl.multiple_of(blk_from(i) * 512, 512), 512)
        for t in range(4):
            rows = pl.ds(t * 256, 256)
            piece = dot(pre[rows, columns], wqkv[i, :, HD:])

            @pl.when(i == 0)
            def _():
                acc[rows, :] = piece

            @pl.when(i > 0)
            def _():
                acc[rows, :] = acc[rows, :] + piece

    def prefix_parts(count, slot_of):
        def one(n, carry):
            prefix_part(slot_of(n))
            return carry

        lax.fori_loop(0, count, one, 0)

    norm_prefix(0)
    arrived(pkr, S_AGY)
    latent_pair = own_and_other(rows_l, unpack_rows(pkr[...].astype(F32)))
    gather_begin(0, latent_pair, gain_l[...])
    spread_cross(1)
    norm_prefix(1)
    gather_step(0, 1)
    spread_cross(2)
    norm_prefix(2)
    gather_step(0, 2)
    spread_cross(3)
    norm_prefix(3)
    gather_step(0, 3)
    wo[0] = perturbed(co, do)
    sqkv[0, :, :HD] = sq[...]
    sqkv[0, :, HD:2 * HD] = sk[...]
    sqkv[0, :, 2 * HD:] = sv[...]
    so[0] = so_in[...]
    gather_step(0, 4)
    prefix_parts(4, lambda n: n + n // 2)
    prefix_parts(2, lambda n: 5 + 2 * n)
    gather_end(0)
    spread_cross(4)

    def latent_slice(u, i):
        columns = pl.ds(pl.multiple_of(blk_from(i) * 512, 512), 512)
        return gat[u, :, :, :, columns].reshape(256, 512)

    def natural(values, width):
        cut = values.reshape(8, 2, 2, 8, width)
        order = jnp.stack([cut[:, cc, yy] for yy in range(2) for cc in range(2)], axis=1)
        return order.reshape(256, width)

    def row_projections(u, weights):
        def one(i, carry):
            piece = dot(latent_slice(u, i), weights[i])

            @pl.when(i == 0)
            def _():
                qacc[...] = piece

            @pl.when(i > 0)
            def _():
                qacc[...] = qacc[...] + piece

            return carry

        lax.fori_loop(0, 8, one, 0)
        return natural(qacc[...], 3 * HD)

    latent_qkv = row_projections(0, wqkv)
    qn[0] = latent_qkv[:, :HD].astype(BF16)
    for i in range(1, 8):
        send(qn.at[0], qn.at[i], S_Q + i, blk_to(i))
    spread_wo(0)
    kn[pl.ds(1024, 256), :] = latent_qkv[:, HD:2 * HD].astype(BF16)
    vt[:, pl.ds(1024, 256)] = latent_qkv[:, 2 * HD:].T.astype(BF16)
    prefix_parts(2, lambda n: 2 + 4 * n)
    for t in range(4):
        rows = pl.ds(t * 256, 256)
        values = acc[rows, :]
        kn[rows, :] = values[:, :HD].astype(BF16)
        vt[:, rows] = values[:, HD:].T.astype(BF16)
    spread_wo(1)

    def attend(i, carry):
        @pl.when(i > 0)
        def _():
            arrived(qn.at[i], S_Q + i)
            arrived(lim.at[i], S_LIM + i)

        source = blk_from(i)
        queries = qn[i]
        seen = lim[i][0:1, :]
        high = jnp.full((8, 256), CLIP, F32)
        for t in range(5):
            s = dot(kn[pl.ds(t * 256, 256), :], queries, 1, 1) * SCALE
            ids = lax.broadcasted_iota(jnp.int32, (256, 256), 0)
            if t < 4:
                allowed = ids + (b * 1024 + t * 256) < seen
            else:
                allowed = ids + b * 256 <= lax.broadcasted_iota(jnp.int32, (256, 256), 1) + source * 256
            s = jnp.where(allowed, s, LOW)
            scores[pl.ds(t * 256, 256), :] = s
            high = jnp.maximum(high, jnp.max(s.reshape(32, 8, 256), axis=0))
        top = jnp.max(high, axis=0, keepdims=True)
        total = jnp.zeros((8, 256), F32)
        weighted = jnp.zeros((HD, 256), F32)
        for t in range(5):
            e = jnp.exp(scores[pl.ds(t * 256, 256), :] - top)
            total = total + jnp.sum(e.reshape(32, 8, 256), axis=0)
            weighted = weighted + dot(vt[:, pl.ds(t * 256, 256)], e.astype(BF16))
        total = jnp.sum(total, axis=0, keepdims=True)
        otx[i] = weighted.astype(BF16)
        first = lax.broadcasted_iota(jnp.int32, (8, 256), 0) == 0
        sttx[i] = jnp.where(first, top, total)

        @pl.when(i > 0)
        def _():
            back = {"blk": source, "grp": g}
            remote(otx.at[i], orx.at[i], S_O + i, back).start()
            remote(sttx.at[i], strx.at[i], S_ST + i, back).start()

        return carry

    lax.fori_loop(0, 4, attend, 0)
    spread_wo(2)
    lax.fori_loop(4, 8, attend, 0)
    spread_wo(3)
    for i in range(1, 8):
        back = {"blk": blk_from(i), "grp": g}
        sent.append(remote(otx.at[i], orx.at[i], S_O + i, back))
        sent.append(remote(sttx.at[i], strx.at[i], S_ST + i, back))
    spread_self(0)

    orx[0] = otx[0]
    strx[0] = sttx[0]
    for i in range(1, 8):
        arrived(orx.at[i], S_O + i)
        arrived(strx.at[i], S_ST + i)
    tops = [strx[i][0:1, :] for i in range(8)]
    top = functools.reduce(jnp.maximum, tops)
    total = jnp.zeros((1, 256), F32)
    weighted = jnp.zeros((HD, 256), F32)
    for i in range(8):
        factor = jnp.exp(tops[i] - top)
        total = total + factor * strx[i][1:2, :]
        weighted = weighted + orx[i].astype(F32) * factor
    mixed[0] = (weighted / total).T.astype(BF16)
    spread_wo(4)
    spread_self(1)

    def half_columns(h):
        return pl.ds(pl.multiple_of(((h + yl) % 2) * HALF, HALF), HALF)

    def project_and_sum(u, weight, between):
        for h in range(2):
            def columns_of(i, carry):
                columns = pl.ds(pl.multiple_of(blk_from(i) * 512, 512), 512)
                y = dot(mixed[u], weight[i]).reshape(8, 2, 2, 8, 512)
                for cc in range(2):
                    part[u, cc, :, :, columns] = y[:, :, cc].reshape(8, 16, 512).astype(BF16)
                return carry

            lax.fori_loop(4 * h, 4 * h + 4, columns_of, 0)
            send(
                part.at[u, 1 - c, :, :, half_columns(h)], sib.at[u, :, :, half_columns(h)],
                S_RSC + 2 * u + h, sibling,
            )

        def chip_sum(zz, h):
            columns = half_columns(h)
            return part[u, c, zz, :, columns].astype(F32) + sib[u, zz, :, columns].astype(F32)

        for k in (4, 3, 2, 1):
            for h, way in ((0, 0), (0, 1), (1, 1), (1, 0)):
                start = 4 if way == h else 3
                if k == 4 and way == h:
                    arrived(sib.at[u, :, :, half_columns(h)], S_RSC + 2 * u + h)
                if k > start:
                    continue
                zz = (z + k) % 8 if way == 0 else (z + 8 - k) % 8
                value = chip_sum(zz, h)
                at = S_RSZ + ((u * 2 + way) * 2 + h) * 5
                if k < start:
                    arrived(rrx.at[u, way, h, k], at + k + 1)
                    value = value + rrx[u, way, h, k].astype(F32)
                rtx[u, way, h, k - 1] = value.astype(BF16)
                send(rtx.at[u, way, h, k - 1], rrx.at[u, way, h, k - 1], at + k, vertical[way])
            between(k)
        halves = []
        for h in range(2):
            value = chip_sum(z, h)
            for way in range(2):
                arrived(rrx.at[u, way, h, 0], S_RSZ + ((u * 2 + way) * 2 + h) * 5 + 1)
                value = value + rrx[u, way, h, 0].astype(F32)
            halves.append(value)
        return jnp.concatenate(
            [jnp.where(yl == 0, halves[0], halves[1]), jnp.where(yl == 0, halves[1], halves[0])], axis=1
        )

    def between_cross(k):
        if k == 4:
            spread_self(2)
        if k == 3:
            spread_so(0)
        if k == 2:
            spread_self(3)
        if k == 1:
            spread_so(1)

    both = project_and_sum(0, wo, between_cross)
    ztx[...] = both.astype(BF16)
    send(ztx, zrx, S_RSY, across)
    arrived(zrx, S_RSY)
    carried = latent_pair + both + zrx[...].astype(F32)
    own_carried = jnp.where(yh == 0, carried[:8], carried[8:])

    gather_begin(1, carried, gain_s[...])
    for k in range(1, 5):
        gather_step(1, k)
        if k == 2:
            spread_so(2)
        if k == 3:
            spread_so(3)
    gather_end(1)
    spread_self(4)

    qkv = row_projections(1, sqkv)
    queries = qkv[:, :HD].astype(BF16)
    k2[0] = qkv[:, HD:2 * HD].astype(BF16)
    v2[0] = qkv[:, 2 * HD:].T.astype(BF16)

    def later(i):
        there = {"blk": jnp.minimum(b + i, 7), "grp": g}
        return (
            remote(k2.at[0], k2.at[i], S_K2 + i, there),
            remote(v2.at[0], v2.at[i], S_V2 + i, there),
        )

    for i in range(1, 8):
        @pl.when(b + i < 8)
        def _():
            for copy in later(i):
                copy.start()

    def absorb(s, values, top, total, weighted):
        new = jnp.maximum(top, jnp.max(s, axis=0, keepdims=True))
        e = jnp.exp(s - new)
        factor = jnp.exp(top - new)
        total = total * factor + jnp.sum(e, axis=0, keepdims=True)
        return new, total, weighted * factor + dot(values, e.astype(BF16))

    s = dot(k2[0], queries, 1, 1) * SCALE
    s = jnp.where(
        lax.broadcasted_iota(jnp.int32, (256, 256), 0) <= lax.broadcasted_iota(jnp.int32, (256, 256), 1),
        s, LOW,
    )
    state = absorb(
        s, v2[0], jnp.full((1, 256), CLIP, F32), jnp.zeros((1, 256), F32), jnp.zeros((HD, 256), F32)
    )

    def self_block(i, state):
        arrived(k2.at[i], S_K2 + i)
        arrived(v2.at[i], S_V2 + i)
        return absorb(dot(k2[i], queries, 1, 1) * SCALE, v2[i], *state)

    top, total, weighted = lax.fori_loop(1, b + 1, self_block, state)
    mixed[1] = (weighted / total).T.astype(BF16)

    spread_so(4)
    both = project_and_sum(1, so, lambda k: None)
    ytx[...] = pack_rows(jnp.where(yh == 0, both[8:], both[:8])).astype(BF16)
    send(ytx, yrx, S_RSY + 1, across)
    arrived(yrx, S_RSY + 1)
    out[...] = own_carried + jnp.where(yh == 0, both[:8], both[8:]) + unpack_rows(yrx[...].astype(F32))

    for i in range(1, 8):
        @pl.when(b + i < 8)
        def _():
            for copy in later(i):
                copy.wait_send()
    for copy in sent:
        copy.wait_send()


def shards(*arguments):
    prefix, latent, limits, gain_p, gain_l, gain_s, *weights = arguments
    vmem = pl.BlockSpec(memory_space=pltpu.VMEM)
    sem = pltpu.SemaphoreType.DMA
    scratch = [
        ((1024, D), BF16),
        ((8, 512, 3 * HD), BF16),
        ((8, HD, 512), BF16),
        ((8, 512, 3 * HD), BF16),
        ((8, HD, 512), BF16),
        ((8, 8, 256), jnp.int32),
        ((8, 256, HD), BF16),
        ((1280, HD), BF16),
        ((HD, 1280), BF16),
        ((1024, 2 * HD), F32),
        ((256, 3 * HD), F32),
        ((1280, 256), F32),
        ((8, HD, 256), BF16),
        ((8, HD, 256), BF16),
        ((8, 8, 256), F32),
        ((8, 8, 256), F32),
        ((2, 256, HD), BF16),
        ((8, 256, HD), BF16),
        ((8, HD, 256), BF16),
        ((16, HALF), BF16),
        ((16, HALF), BF16),
        ((2, 8, 2, 16, D), BF16),
        ((2, 2, 8, 16, D), BF16),
        ((2, 8, 16, D), BF16),
        ((2, 2, 2, 4, 16, HALF), BF16),
        ((2, 2, 2, 4, 16, HALF), BF16),
        ((16, HALF), BF16),
        ((16, HALF), BF16),
        ((16, D), BF16),
        ((16, D), BF16),
    ]
    return pl.pallas_call(
        layer_kernel,
        out_shape=jax.ShapeDtypeStruct((8, D), F32),
        in_specs=[pl.BlockSpec(memory_space=pl.ANY)] + [vmem] * 17,
        out_specs=vmem,
        scratch_shapes=[pltpu.VMEM(shape, dtype) for shape, dtype in scratch]
        + [sem((N_SEM,)), sem((N_SEM,)), sem((4,))],
        compiler_params=pltpu.CompilerParams(
            collective_id=0, has_side_effects=True, vmem_limit_bytes=56 * 1024 * 1024
        ),
        name="layer",
    )(
        prefix, latent, limits.reshape(1, -1),
        gain_p.reshape(1, -1), gain_l.reshape(1, -1), gain_s.reshape(1, -1), *weights,
    )


def solution(mesh):
    return jax.shard_map(
        shards,
        mesh=mesh,
        in_specs=(
            P("blk", None), P(("blk", "grp"), None), P("blk"), P(), P(), P(),
            P("blk", "grp"), P("blk", "grp"), P("blk", "grp"), P("grp", "blk"),
            P("blk", "grp"), P("blk", "grp"), P("blk", "grp"), P("grp", "blk"),
            P("blk", "grp"), P("blk", "grp"), P("blk", "grp"), P("grp", "blk"),
        ),
        out_specs=P(("blk", "grp"), None),
        check_vma=False,
    )
```

```python
import functools

import jax
import jax.numpy as jnp
from jax import lax
from jax.experimental import pallas as pl
from jax.experimental.pallas import tpu as pltpu
from jax.sharding import PartitionSpec as P

D = 4096
HD = 128
HALF = D // 2
EPS = 1e-05
SCALE = HD ** (-0.5)
LOW = -1e30
CLIP = -1e20
MESH = pl.DeviceIdType.MESH
F32 = jnp.float32
BF16 = jnp.bfloat16

N_SEM = 0


def _places(count):
    global N_SEM
    first = N_SEM
    N_SEM += count
    return first


S_W = _places(4 * 10)
S_WO = _places(10)
S_SQKV = _places(10)
S_SO = _places(10)
S_LIM = _places(8)
S_Q = _places(8)
S_O = _places(8)
S_ST = _places(8)
S_KV2 = _places(10)
S_AGY = _places(2)
S_AGZ = _places(2 * 2 * 5)
S_AGC = _places(2 * 8)
S_RSC = _places(4)
S_RSZ = _places(2 * 2 * 2 * 5)
S_RSY = _places(2)


def rms_rows(values, gain):
    inverse = lax.rsqrt(jnp.sum(values * values, axis=1, keepdims=True) * (1.0 / D) + EPS)
    return values * inverse * gain


def pack_rows(rows):
    return jnp.concatenate([rows[:, :HALF], rows[:, HALF:]], axis=0)


def unpack_rows(packed):
    return jnp.concatenate([packed[:8], packed[8:]], axis=1)


def dot(a, b, ca=1, cb=0):
    return lax.dot_general(a, b, (((ca,), (cb,)), ((), ())), preferred_element_type=F32)


def layer_kernel(
    prefix, latent, limits, gain_p, gain_l, gain_s,
    cq, ck, cv, co, dq, dk, dv, do, sq, sk, sv, so_in,
    out,
    pre, wqkv, wo, sqkv, so, lim, qn, kn, vt, acc, scores,
    otx, orx, sttx, strx, mixed, kv2, top2, total2, weighted2,
    pk, pkr, gat, part, sib, rtx, rrx, ytx, yrx, ztx, zrx,
    ss, rs, ls,
):
    b = lax.axis_index("blk")
    g = lax.axis_index("grp")
    x, yl = b % 4, b // 4
    z, yh, c = g // 4, (g // 2) % 2, g % 2

    def blk_to(i):
        return {"blk": ((yl + i // 4) % 2) * 4 + (x + i % 4) % 4, "grp": g}

    def blk_from(i):
        return ((yl + i // 4) % 2) * 4 + (x + 4 - i % 4) % 4

    def grp_at(zz, yy, cc):
        return {"blk": b, "grp": (zz * 2 + yy) * 2 + cc}

    sibling = grp_at(z, yh, 1 - c)
    across = grp_at(z, 1 - yh, c)
    above = grp_at((z + 1) % 8, yh, c)
    below = grp_at((z + 7) % 8, yh, c)
    vertical = (above, below)

    def remote(src, dst, place, device):
        return pltpu.make_async_remote_copy(
            src_ref=src, dst_ref=dst, send_sem=ss.at[place], recv_sem=rs.at[place],
            device_id=device, device_id_type=MESH,
        )

    sent = []

    def send(src, dst, place, device):
        copy = remote(src, dst, place, device)
        copy.start()
        sent.append(copy)

    def arrived(dst, place):
        remote(dst, dst, place, sibling).wait_recv()

    barrier = pltpu.get_barrier_semaphore()
    for i in range(1, 8):
        pl.semaphore_signal(barrier, inc=1, device_id=blk_to(i), device_id_type=MESH)
    for device in (sibling, across, above, below):
        pl.semaphore_signal(barrier, inc=1, device_id=device, device_id_type=MESH)

    loads = [
        pltpu.make_async_copy(prefix.at[pl.ds(t * 256, 256)], pre.at[pl.ds(t * 256, 256)], ls.at[t])
        for t in range(4)
    ]
    for load in loads:
        load.start()

    def perturbed(weight, delta):
        return (weight[...].astype(F32) + delta[...].astype(F32)).astype(BF16)

    rows_l = latent[...].astype(F32)
    pk[...] = pack_rows(rows_l).astype(BF16)
    lim[0] = jnp.broadcast_to(limits[...], (8, 256))
    wqkv[b, :, :HD] = perturbed(cq, dq)
    wqkv[b, :, HD:2 * HD] = perturbed(ck, dk)
    wqkv[b, :, 2 * HD:] = perturbed(cv, dv)
    pl.semaphore_wait(barrier, 11)

    right, left, beside = blk_to(1), blk_to(3), blk_to(4)

    def spread(buf, start, rows, place, y_first, stage):
        def here(i, piece=None):
            if piece is None:
                return buf.at[blk_from(i), pl.ds(start, rows)]
            return buf.at[blk_from(i), pl.ds(start + piece * (rows // 2), rows // 2)]

        if stage == 0:
            send(here(0), here(0), place + 4, beside)
            send(here(0), here(0), place + 1, right)
            send(here(0), here(0), place + 3, left)
        elif y_first and stage == 1:
            arrived(here(4), place + 4)
            send(here(4), here(4), place + 5, right)
            send(here(4), here(4), place + 7, left)
        elif y_first and stage == 2:
            arrived(here(1), place + 1)
            send(here(1, 0), here(1, 0), place + 2, right)
            arrived(here(3), place + 3)
            send(here(3, 1), here(3, 1), place + 8, left)
        elif y_first and stage == 3:
            arrived(here(5), place + 5)
            send(here(5, 0), here(5, 0), place + 6, right)
            arrived(here(7), place + 7)
            send(here(7, 1), here(7, 1), place + 9, left)
        elif y_first and stage == 4:
            arrived(here(2, 0), place + 2)
            arrived(here(2, 1), place + 8)
        elif y_first:
            arrived(here(6, 0), place + 6)
            arrived(here(6, 1), place + 9)
        elif stage == 1:
            arrived(here(1), place + 1)
            send(here(1, 0), here(1, 0), place + 2, right)
            send(here(1), here(1), place + 5, beside)
            arrived(here(3), place + 3)
            send(here(3, 1), here(3, 1), place + 8, left)
            send(here(3), here(3), place + 7, beside)
        elif stage == 2:
            arrived(here(2, 0), place + 2)
            arrived(here(2, 1), place + 8)
            send(here(2), here(2), place + 6, beside)
        elif stage == 5:
            for i in (4, 5, 7, 6):
                arrived(here(i), place + i)

    def spread_cross(stage, parts):
        for n in parts:
            spread(wqkv, n * 128, 128, S_W + 10 * n, n % 2 == 1, stage)

    def spread_self(stage):
        spread(sqkv, 0, 512, S_SQKV, True, stage)

    def spread_wo(stage):
        spread(wo, 0, HD, S_WO, True, stage)

    def spread_so(stage):
        spread(so, 0, HD, S_SO, True, stage)

    def own_and_other(own, other):
        return jnp.concatenate([jnp.where(yh == 0, own, other), jnp.where(yh == 0, other, own)], axis=0)

    def gather_begin(u, rows, gain):
        gat[u, z, c] = rms_rows(rows, gain).astype(BF16)
        own = gat.at[u, z, c]
        for way in range(2):
            send(own, own, S_AGZ + (u * 2 + way) * 5 + 1, vertical[way])
        send(own, own, S_AGC + u * 8, sibling)

    def gather_step(u, k):
        for way in range(2):
            zz = (z + 8 - k) % 8 if way == 0 else (z + k) % 8
            chunk = gat.at[u, zz, c]
            if k < 4:
                arrived(chunk, S_AGZ + (u * 2 + way) * 5 + k)
                onward = chunk
                if k == 3:
                    onward = gat.at[u, zz, c, :, pl.ds(way * HALF, HALF)]
                send(onward, onward, S_AGZ + (u * 2 + way) * 5 + k + 1, vertical[way])
                send(chunk, chunk, S_AGC + u * 8 + (k if way == 0 else 8 - k), sibling)
            else:
                piece = gat.at[u, zz, c, :, pl.ds(way * HALF, HALF)]
                arrived(piece, S_AGZ + (u * 2 + way) * 5 + 4)
        if k == 4:
            chunk = gat.at[u, (z + 4) % 8, c]
            send(chunk, chunk, S_AGC + u * 8 + 4, sibling)

    def gather_end(u):
        for k in range(8):
            arrived(gat.at[u, (z + 8 - k) % 8, 1 - c], S_AGC + u * 8 + k)

    send(pk, pkr, S_AGY, across)
    spread_cross(0, (0, 1, 2, 3))
    for i in range(1, 8):
        send(lim.at[0], lim.at[i], S_LIM + i, blk_to(i))

    def norm_prefix(t):
        if t % 2 == 0:
            loads[t // 2].wait()

        def tile(n, carry):
            rows = pl.ds(pl.multiple_of(t * 128 + n * 16, 16), 16)
            pre[rows, :] = rms_rows(pre[rows, :].astype(F32), gain_p[...]).astype(BF16)
            return carry

        lax.fori_loop(0, 8, tile, 0)

    def prefix_part(row, first):
        columns = pl.ds(pl.multiple_of(row * HALF, HALF), HALF)
        weights = wqkv[pl.ds(row * 4, 4), :, HD:].reshape(HALF, 2 * HD)
        for t in range(2):
            rows = pl.ds(t * 512, 512)
            piece = dot(pre[rows, columns], weights)
            acc[rows, :] = piece if first else acc[rows, :] + piece

    def latent_rows(u):
        return gat[u].reshape(256, D)

    def natural(values, width):
        cut = values.reshape(8, 2, 2, 8, width)
        order = jnp.stack([cut[:, cc, yy] for yy in range(2) for cc in range(2)], axis=1)
        return order.reshape(256, width)

    norm_prefix(0)
    arrived(pkr, S_AGY)
    latent_pair = own_and_other(rows_l, unpack_rows(pkr[...].astype(F32)))
    gather_begin(0, latent_pair, gain_l[...])
    norm_prefix(1)
    spread_cross(1, (0, 1))
    norm_prefix(2)
    gather_step(0, 1)
    spread_cross(1, (2, 3))
    norm_prefix(3)
    spread_cross(2, (0, 1))
    gather_step(0, 2)
    norm_prefix(4)
    spread_cross(2, (2, 3))
    norm_prefix(5)
    gather_step(0, 3)
    spread_cross(3, (0, 1))
    norm_prefix(6)
    gather_step(0, 4)
    spread_cross(3, (2, 3))
    norm_prefix(7)
    wo[b] = perturbed(co, do)
    sqkv[b, :, :HD] = sq[...]
    sqkv[b, :, HD:2 * HD] = sk[...]
    sqkv[b, :, 2 * HD:] = sv[...]
    so[b] = so_in[...]
    gather_end(0)
    spread_cross(4, (0, 1, 2, 3))
    prefix_part(yl, True)
    spread_cross(5, (0, 1, 2, 3))
    qn[0] = natural(dot(latent_rows(0), wqkv[:, :, :HD].reshape(D, HD)), HD).astype(BF16)
    for i in range(1, 8):
        send(qn.at[0], qn.at[i], S_Q + i, blk_to(i))
    spread_wo(0)
    prefix_part(1 - yl, False)
    latent_kv = natural(dot(latent_rows(0), wqkv[:, :, HD:].reshape(D, 2 * HD)), 2 * HD)
    for t in range(5):
        rows = pl.ds(t * 256, 256)
        values = acc[rows, :] if t < 4 else latent_kv
        kn[rows, :] = values[:, :HD].astype(BF16)
        vt[:, rows] = values[:, HD:].T.astype(BF16)

    def attend(n, carry):
        i = (n + 1) % 8

        @pl.when(i > 0)
        def _():
            arrived(qn.at[i], S_Q + i)
            arrived(lim.at[i], S_LIM + i)

        source = blk_from(i)
        queries = qn[i]
        seen = lim[i][0:1, :]
        high = jnp.full((8, 256), CLIP, F32)
        for t in range(5):
            s = dot(kn[pl.ds(t * 256, 256), :], queries, 1, 1) * SCALE
            ids = lax.broadcasted_iota(jnp.int32, (256, 256), 0)
            if t < 4:
                allowed = ids + (b * 1024 + t * 256) < seen
            else:
                allowed = ids + b * 256 <= lax.broadcasted_iota(jnp.int32, (256, 256), 1) + source * 256
            s = jnp.where(allowed, s, LOW)
            scores[pl.ds(t * 256, 256), :] = s
            high = jnp.maximum(high, jnp.max(s.reshape(32, 8, 256), axis=0))
        top = jnp.max(high, axis=0, keepdims=True)
        total = jnp.zeros((8, 256), F32)
        weighted = jnp.zeros((HD, 256), F32)
        for t in range(5):
            e = jnp.exp(scores[pl.ds(t * 256, 256), :] - top)
            total = total + jnp.sum(e.reshape(32, 8, 256), axis=0)
            weighted = weighted + dot(vt[:, pl.ds(t * 256, 256)], e.astype(BF16))
        total = jnp.sum(total, axis=0, keepdims=True)
        otx[i] = weighted.astype(BF16)
        first = lax.broadcasted_iota(jnp.int32, (8, 256), 0) == 0
        sttx[i] = jnp.where(first, top, total)

        @pl.when(i > 0)
        def _():
            back = {"blk": source, "grp": g}
            remote(otx.at[i], orx.at[i], S_O + i, back).start()
            remote(sttx.at[i], strx.at[i], S_ST + i, back).start()

        return carry

    lax.fori_loop(0, 3, attend, 0)
    spread_wo(1)
    spread_wo(2)
    lax.fori_loop(3, 8, attend, 0)
    spread_wo(3)
    for i in range(1, 8):
        back = {"blk": blk_from(i), "grp": g}
        sent.append(remote(otx.at[i], orx.at[i], S_O + i, back))
        sent.append(remote(sttx.at[i], strx.at[i], S_ST + i, back))
    orx[0] = otx[0]
    strx[0] = sttx[0]
    for i in range(1, 8):
        arrived(orx.at[i], S_O + i)
        arrived(strx.at[i], S_ST + i)
    tops = [strx[i][0:1, :] for i in range(8)]
    top = functools.reduce(jnp.maximum, tops)
    total = jnp.zeros((1, 256), F32)
    weighted = jnp.zeros((HD, 256), F32)
    for i in range(8):
        factor = jnp.exp(tops[i] - top)
        total = total + factor * strx[i][1:2, :]
        weighted = weighted + orx[i].astype(F32) * factor
    mixed[0] = (weighted / total).T.astype(BF16)
    spread_self(0)
    spread_wo(4)
    spread_wo(5)

    def half_columns(h):
        return pl.ds(h * HALF, HALF)

    def project_and_sum(u, weight, between):
        for h in range(2):
            def columns_of(i, carry):
                columns = pl.ds(pl.multiple_of(i * 512, 512), 512)
                y = dot(mixed[u], weight[i]).reshape(8, 2, 2, 8, 512)
                for cc in range(2):
                    part[u, cc, :, :, columns] = y[:, :, cc].reshape(8, 16, 512).astype(BF16)
                return carry

            lax.fori_loop(4 * h, 4 * h + 4, columns_of, 0)
            send(
                part.at[u, 1 - c, :, :, half_columns(h)], sib.at[u, :, :, half_columns(h)],
                S_RSC + 2 * u + h, sibling,
            )

        def chip_sum(zz, h):
            columns = half_columns(h)
            return part[u, c, zz, :, columns].astype(F32) + sib[u, zz, :, columns].astype(F32)

        for k in (4, 3, 2, 1):
            for h, way in ((0, 0), (0, 1), (1, 1), (1, 0)):
                start = 4 if way == h else 3
                if k == 4 and way == h:
                    arrived(sib.at[u, :, :, half_columns(h)], S_RSC + 2 * u + h)
                if k > start:
                    continue
                zz = (z + k) % 8 if way == 0 else (z + 8 - k) % 8
                value = chip_sum(zz, h)
                at = S_RSZ + ((u * 2 + way) * 2 + h) * 5
                if k < start:
                    arrived(rrx.at[u, way, h, k], at + k + 1)
                    value = value + rrx[u, way, h, k].astype(F32)
                rtx[u, way, h, k - 1] = value.astype(BF16)
                send(rtx.at[u, way, h, k - 1], rrx.at[u, way, h, k - 1], at + k, vertical[way])
            between(k)
        halves = []
        for h in range(2):
            value = chip_sum(z, h)
            for way in range(2):
                arrived(rrx.at[u, way, h, 0], S_RSZ + ((u * 2 + way) * 2 + h) * 5 + 1)
                value = value + rrx[u, way, h, 0].astype(F32)
            halves.append(value)
        return jnp.concatenate(halves, axis=1)

    def between_cross(k):
        if k == 2:
            spread_self(1)
        if k == 1:
            spread_self(2)

    both = project_and_sum(0, wo, between_cross)
    ztx[...] = both.astype(BF16)
    send(ztx, zrx, S_RSY, across)
    spread_so(0)
    arrived(zrx, S_RSY)
    carried = latent_pair + both + zrx[...].astype(F32)
    own_carried = jnp.where(yh == 0, carried[:8], carried[8:])

    gather_begin(1, carried, gain_s[...])
    for k in range(1, 5):
        gather_step(1, k)
        if k == 1:
            spread_self(3)
        if k == 3:
            spread_so(1)
            spread_so(2)
    spread_so(3)
    gather_end(1)
    spread_self(4)
    spread_self(5)

    qkv = natural(dot(latent_rows(1), sqkv[...].reshape(D, 3 * HD)), 3 * HD)
    queries = qkv[:, :HD].astype(BF16)
    kv2[b] = qkv[:, HD:].astype(BF16)

    def spread_keyval(stage):
        spread(kv2, 0, 256, S_KV2, True, stage)

    def absorb(source, own):
        block = kv2[source]
        s = dot(block[:, :HD], queries, 1, 1) * SCALE
        if own:
            ids = lax.broadcasted_iota(jnp.int32, (256, 256), 0)
            s = jnp.where(ids <= lax.broadcasted_iota(jnp.int32, (256, 256), 1), s, LOW)
        top = jnp.max(s, axis=0, keepdims=True)
        if not own:
            top = jnp.maximum(top, top2[...])
        e = jnp.exp(s - top)
        total = jnp.sum(e, axis=0, keepdims=True)
        weighted = dot(block[:, HD:], e.astype(BF16), 0, 0)
        if not own:
            factor = jnp.exp(top2[...] - top)
            total = total + total2[...] * factor
            weighted = weighted + weighted2[...] * factor
        top2[...] = top
        total2[...] = total
        weighted2[...] = weighted

    def absorb_earlier(*slots):
        for i in slots:
            @pl.when(blk_from(i) < b)
            def _():
                absorb(blk_from(i), False)

    spread_keyval(0)
    absorb(b, True)
    spread_keyval(1)
    spread_keyval(2)
    absorb_earlier(4, 1, 3)
    spread_keyval(3)
    absorb_earlier(5, 7)
    spread_keyval(4)
    absorb_earlier(2)
    spread_keyval(5)
    absorb_earlier(6)
    mixed[1] = (weighted2[...] / total2[...]).T.astype(BF16)

    spread_so(4)
    spread_so(5)
    both = project_and_sum(1, so, lambda k: None)
    ytx[...] = pack_rows(jnp.where(yh == 0, both[8:], both[:8])).astype(BF16)
    send(ytx, yrx, S_RSY + 1, across)
    arrived(yrx, S_RSY + 1)
    out[...] = own_carried + jnp.where(yh == 0, both[:8], both[8:]) + unpack_rows(yrx[...].astype(F32))

    for copy in sent:
        copy.wait_send()


def shards(*arguments):
    prefix, latent, limits, gain_p, gain_l, gain_s, *weights = arguments
    vmem = pl.BlockSpec(memory_space=pltpu.VMEM)
    sem = pltpu.SemaphoreType.DMA
    scratch = [
        ((1024, D), BF16),
        ((8, 512, 3 * HD), BF16),
        ((8, HD, 512), BF16),
        ((8, 512, 3 * HD), BF16),
        ((8, HD, 512), BF16),
        ((8, 8, 256), jnp.int32),
        ((8, 256, HD), BF16),
        ((1280, HD), BF16),
        ((HD, 1280), BF16),
        ((1024, 2 * HD), F32),
        ((1280, 256), F32),
        ((8, HD, 256), BF16),
        ((8, HD, 256), BF16),
        ((8, 8, 256), F32),
        ((8, 8, 256), F32),
        ((2, 256, HD), BF16),
        ((8, 256, 2 * HD), BF16),
        ((1, 256), F32),
        ((1, 256), F32),
        ((HD, 256), F32),
        ((16, HALF), BF16),
        ((16, HALF), BF16),
        ((2, 8, 2, 16, D), BF16),
        ((2, 2, 8, 16, D), BF16),
        ((2, 8, 16, D), BF16),
        ((2, 2, 2, 4, 16, HALF), BF16),
        ((2, 2, 2, 4, 16, HALF), BF16),
        ((16, HALF), BF16),
        ((16, HALF), BF16),
        ((16, D), BF16),
        ((16, D), BF16),
    ]
    return pl.pallas_call(
        layer_kernel,
        out_shape=jax.ShapeDtypeStruct((8, D), F32),
        in_specs=[pl.BlockSpec(memory_space=pl.ANY)] + [vmem] * 17,
        out_specs=vmem,
        scratch_shapes=[pltpu.VMEM(shape, dtype) for shape, dtype in scratch]
        + [sem((N_SEM,)), sem((N_SEM,)), sem((4,))],
        compiler_params=pltpu.CompilerParams(
            collective_id=0, has_side_effects=True, vmem_limit_bytes=56 * 1024 * 1024
        ),
        name="layer",
    )(
        prefix, latent, limits.reshape(1, -1),
        gain_p.reshape(1, -1), gain_l.reshape(1, -1), gain_s.reshape(1, -1), *weights,
    )


def solution(mesh):
    return jax.shard_map(
        shards,
        mesh=mesh,
        in_specs=(
            P("blk", None), P(("blk", "grp"), None), P("blk"), P(), P(), P(),
            P("blk", "grp"), P("blk", "grp"), P("blk", "grp"), P("grp", "blk"),
            P("blk", "grp"), P("blk", "grp"), P("blk", "grp"), P("grp", "blk"),
            P("blk", "grp"), P("blk", "grp"), P("blk", "grp"), P("grp", "blk"),
        ),
        out_specs=P(("blk", "grp"), None),
        check_vma=False,
    )
```

```python
import functools

import jax
import jax.numpy as jnp
from jax import lax
from jax.experimental import pallas as pl
from jax.experimental.pallas import tpu as pltpu
from jax.sharding import PartitionSpec as P

D = 4096
HD = 128
HALF = D // 2
EPS = 1e-05
SCALE = HD ** (-0.5)
LOW = -1e30
CLIP = -1e20
MESH = pl.DeviceIdType.MESH
F32 = jnp.float32
BF16 = jnp.bfloat16

N_SEM = 0


def _places(count):
    global N_SEM
    first = N_SEM
    N_SEM += count
    return first


S_W = _places(4 * 10)
S_WO = _places(10)
S_SQKV = _places(10)
S_SO = _places(10)
S_LIM = _places(8)
S_Q = _places(8)
S_O = _places(8)
S_ST = _places(8)
S_KV2 = _places(4 * 10)
S_AGY = _places(2)
S_AGZ = _places(2 * 2 * 5 * 2)
S_AGC = _places(2 * 8 * 2)
S_RSC = _places(4)
S_RSZ = _places(2 * 2 * 2 * 5)
S_RSY = _places(4)


def rms_rows(values, gain):
    inverse = lax.rsqrt(jnp.sum(values * values, axis=1, keepdims=True) * (1.0 / D) + EPS)
    return values * inverse * gain


def pack_rows(rows):
    return jnp.concatenate([rows[:, :HALF], rows[:, HALF:]], axis=0)


def unpack_rows(packed):
    return jnp.concatenate([packed[:8], packed[8:]], axis=1)


def dot(a, b, ca=1, cb=0):
    return lax.dot_general(a, b, (((ca,), (cb,)), ((), ())), preferred_element_type=F32)


def layer_kernel(
    prefix, latent, limits, gain_p, gain_l, gain_s,
    cq, ck, cv, co, dq, dk, dv, do, sq, sk, sv, so_in,
    out,
    raw, raw_o, pre, wqkv, wo, sqkv, so, lim, qn, kn, vt, acc, scores,
    otx, orx, sttx, strx, mixed, kv2, top2, total2, weighted2,
    pk, pkr, gat, part, sib, rtx, rrx, ytx, yrx, ztx, zrx, latent16, carried16,
    ss, rs, ls,
):
    b = lax.axis_index("blk")
    g = lax.axis_index("grp")
    x, yl = b % 4, b // 4
    z, yh, c = g // 4, (g // 2) % 2, g % 2

    def blk_to(i):
        return {"blk": ((yl + i // 4) % 2) * 4 + (x + i % 4) % 4, "grp": g}

    def blk_from(i):
        return ((yl + i // 4) % 2) * 4 + (x + 4 - i % 4) % 4

    def grp_at(zz, yy, cc):
        return {"blk": b, "grp": (zz * 2 + yy) * 2 + cc}

    sibling = grp_at(z, yh, 1 - c)
    across = grp_at(z, 1 - yh, c)
    above = grp_at((z + 1) % 8, yh, c)
    below = grp_at((z + 7) % 8, yh, c)
    vertical = (above, below)

    def remote(src, dst, place, device):
        return pltpu.make_async_remote_copy(
            src_ref=src, dst_ref=dst, send_sem=ss.at[place], recv_sem=rs.at[place],
            device_id=device, device_id_type=MESH,
        )

    sent = []

    def send(src, dst, place, device):
        copy = remote(src, dst, place, device)
        copy.start()
        sent.append(copy)

    def arrived(dst, place):
        remote(dst, dst, place, sibling).wait_recv()

    barrier = pltpu.get_barrier_semaphore()
    for i in range(1, 8):
        pl.semaphore_signal(barrier, inc=1, device_id=blk_to(i), device_id_type=MESH)
    for device in (sibling, across, above, below):
        pl.semaphore_signal(barrier, inc=1, device_id=device, device_id_type=MESH)

    loads = [
        pltpu.make_async_copy(prefix.at[pl.ds(t * 256, 256)], pre.at[pl.ds(t * 256, 256)], ls.at[t])
        for t in range(4)
    ]
    raw_loads = [
        pltpu.make_async_copy(source, raw.at[n], ls.at[4 + n])
        for n, source in enumerate((cq, ck, cv, dq, dk, dv))
    ] + [
        pltpu.make_async_copy(source, raw_o.at[n], ls.at[10 + n]) for n, source in enumerate((co, do))
    ]
    self_loads = [
        pltpu.make_async_copy(source, sqkv.at[b, :, pl.ds(n * HD, HD)], ls.at[12 + n])
        for n, source in enumerate((sq, sk, sv))
    ] + [pltpu.make_async_copy(so_in, so.at[b], ls.at[15])]
    for load in raw_loads + self_loads:
        load.start()
    for load in loads:
        load.start()

    def perturbed(weight, delta):
        return (weight.astype(F32) + delta.astype(F32)).astype(BF16)

    rows_l = latent[...].astype(F32)
    pk[...] = pack_rows(rows_l).astype(BF16)
    lim[0] = jnp.broadcast_to(limits[...], (8, 256))
    for load in raw_loads:
        load.wait()
    for n in range(3):
        wqkv[b, :, n * HD:(n + 1) * HD] = perturbed(raw[n], raw[n + 3])
    pl.semaphore_wait(barrier, 11)

    right, left, beside = blk_to(1), blk_to(3), blk_to(4)

    def spread(buf, start, rows, place, y_first, stage):
        def here(i, piece=None):
            if piece is None:
                return buf.at[blk_from(i), pl.ds(start, rows)]
            return buf.at[blk_from(i), pl.ds(start + piece * (rows // 2), rows // 2)]

        if stage == 0:
            send(here(0), here(0), place + 4, beside)
            send(here(0), here(0), place + 1, right)
            send(here(0), here(0), place + 3, left)
        elif y_first and stage == 1:
            arrived(here(4), place + 4)
            send(here(4), here(4), place + 5, right)
            send(here(4), here(4), place + 7, left)
        elif y_first and stage == 2:
            arrived(here(1), place + 1)
            send(here(1, 0), here(1, 0), place + 2, right)
            arrived(here(3), place + 3)
            send(here(3, 1), here(3, 1), place + 8, left)
        elif y_first and stage == 3:
            arrived(here(5), place + 5)
            send(here(5, 0), here(5, 0), place + 6, right)
            arrived(here(7), place + 7)
            send(here(7, 1), here(7, 1), place + 9, left)
        elif y_first and stage == 4:
            arrived(here(2, 0), place + 2)
            arrived(here(2, 1), place + 8)
        elif y_first:
            arrived(here(6, 0), place + 6)
            arrived(here(6, 1), place + 9)
        elif stage == 1:
            arrived(here(1), place + 1)
            send(here(1, 0), here(1, 0), place + 2, right)
            send(here(1), here(1), place + 5, beside)
            arrived(here(3), place + 3)
            send(here(3, 1), here(3, 1), place + 8, left)
            send(here(3), here(3), place + 7, beside)
        elif stage == 2:
            arrived(here(2, 0), place + 2)
            arrived(here(2, 1), place + 8)
            send(here(2), here(2), place + 6, beside)
        elif stage == 5:
            for i in (4, 5, 7, 6):
                arrived(here(i), place + i)

    def spread_cross(stage, parts):
        for n in parts:
            start, rows = ((0, 96), (96, 160), (256, 128), (384, 128))[n]
            spread(wqkv, start, rows, S_W + 10 * n, n % 2 == 1, stage)

    def spread_self(stage):
        spread(sqkv, 0, 512, S_SQKV, True, stage)

    def spread_wo(stage):
        spread(wo, 0, HD, S_WO, True, stage)

    def spread_so(stage):
        spread(so, 0, HD, S_SO, True, stage)

    def own_and_other(own, other):
        return jnp.concatenate([jnp.where(yh == 0, own, other), jnp.where(yh == 0, other, own)], axis=0)

    def half_columns(h):
        return pl.ds(h * HALF, HALF)

    def gather_begin(u, rows, gain):
        gat[u, z, c] = rms_rows(rows, gain).astype(BF16)
        for n in range(2):
            for way in range(2):
                h = n if way == 0 else 1 - n
                own = gat.at[u, z, c, :, half_columns(h)]
                send(own, own, S_AGZ + ((u * 2 + way) * 5 + 1) * 2 + h, vertical[way])
        for h in range(2):
            own = gat.at[u, z, c, :, half_columns(h)]
            send(own, own, S_AGC + u * 16 + h, sibling)

    def gather_step(u, k):
        for n in range(2):
            for way in range(2):
                h = n if way == 0 else 1 - n
                if k == 4 and n == 1:
                    continue
                zz = (z + 8 - k) % 8 if way == 0 else (z + k) % 8
                chunk = gat.at[u, zz, c, :, half_columns(h)]
                arrived(chunk, S_AGZ + ((u * 2 + way) * 5 + k) * 2 + h)
                if k < 3 or k == 3 and n == 0:
                    send(chunk, chunk, S_AGZ + ((u * 2 + way) * 5 + k + 1) * 2 + h, vertical[way])
                send(chunk, chunk, S_AGC + u * 16 + (k if way == 0 else 8 - k) * 2 + h, sibling)

    def gather_end(u):
        for k in range(8):
            for h in range(2):
                arrived(gat.at[u, (z + 8 - k) % 8, 1 - c, :, half_columns(h)], S_AGC + u * 16 + 2 * k + h)

    send(pk, pkr, S_AGY, across)
    spread_cross(0, (0, 1, 2, 3))
    for i in range(1, 8):
        send(lim.at[0], lim.at[i], S_LIM + i, blk_to(i))

    def norm_prefix(t):
        if t % 2 == 0:
            loads[t // 2].wait()

        def tile(n, carry):
            rows = pl.ds(pl.multiple_of(t * 128 + n * 16, 16), 16)
            pre[rows, :] = rms_rows(pre[rows, :].astype(F32), gain_p[...]).astype(BF16)
            return carry

        lax.fori_loop(0, 8, tile, 0)

    def prefix_part(row, first):
        columns = pl.ds(pl.multiple_of(row * HALF, HALF), HALF)
        weights = wqkv[pl.ds(row * 4, 4), :, HD:].reshape(HALF, 2 * HD)
        for t in range(2):
            rows = pl.ds(t * 512, 512)
            piece = dot(pre[rows, columns], weights)
            acc[rows, :] = piece if first else acc[rows, :] + piece

    def latent_rows(u):
        return gat[u].reshape(256, D)

    def natural(values, width):
        cut = values.reshape(8, 2, 2, 8, width)
        order = jnp.stack([cut[:, cc, yy] for yy in range(2) for cc in range(2)], axis=1)
        return order.reshape(256, width)

    norm_prefix(0)
    arrived(pkr, S_AGY)
    latent16[...] = own_and_other(rows_l, unpack_rows(pkr[...].astype(F32)))
    gather_begin(0, latent16[...], gain_l[...])
    norm_prefix(1)
    spread_cross(1, (0, 1))
    gather_step(0, 1)
    norm_prefix(2)
    gather_step(0, 2)
    spread_cross(1, (2, 3))
    norm_prefix(3)
    spread_cross(2, (0, 1))
    norm_prefix(4)
    gather_step(0, 3)
    spread_cross(2, (2, 3))
    norm_prefix(5)
    spread_cross(3, (0, 1))
    gather_step(0, 4)
    norm_prefix(6)
    spread_cross(3, (2, 3))
    norm_prefix(7)
    wo[b] = perturbed(raw_o[0], raw_o[1])
    spread_wo(0)
    spread_cross(4, (0, 1, 2, 3))
    prefix_part(yl, True)
    gather_end(0)
    spread_cross(5, (0, 1, 2, 3))
    qn[0] = natural(dot(latent_rows(0), wqkv[:, :, :HD].reshape(D, HD)), HD).astype(BF16)
    for i in range(1, 8):
        send(qn.at[0], qn.at[i], S_Q + i, blk_to(i))
    spread_wo(1)
    prefix_part(1 - yl, False)
    latent_kv = natural(dot(latent_rows(0), wqkv[:, :, HD:].reshape(D, 2 * HD)), 2 * HD)
    for t in range(5):
        rows = pl.ds(t * 256, 256)
        values = acc[rows, :] if t < 4 else latent_kv
        kn[rows, :] = values[:, :HD].astype(BF16)
        vt[:, rows] = values[:, HD:].T.astype(BF16)

    def attend(n, carry):
        i = (n + 1) % 8

        @pl.when(i > 0)
        def _():
            arrived(qn.at[i], S_Q + i)
            arrived(lim.at[i], S_LIM + i)

        source = blk_from(i)
        queries = qn[i]
        seen = lim[i][0:1, :]
        high = jnp.full((8, 256), CLIP, F32)
        for t in range(5):
            s = dot(kn[pl.ds(t * 256, 256), :], queries, 1, 1) * SCALE
            ids = lax.broadcasted_iota(jnp.int32, (256, 256), 0)
            if t < 4:
                allowed = ids + (b * 1024 + t * 256) < seen
            else:
                allowed = ids + b * 256 <= lax.broadcasted_iota(jnp.int32, (256, 256), 1) + source * 256
            s = jnp.where(allowed, s, LOW)
            scores[pl.ds(t * 256, 256), :] = s
            high = jnp.maximum(high, jnp.max(s.reshape(32, 8, 256), axis=0))
        top = jnp.max(high, axis=0, keepdims=True)
        total = jnp.zeros((8, 256), F32)
        weighted = jnp.zeros((HD, 256), F32)
        for t in range(5):
            e = jnp.exp(scores[pl.ds(t * 256, 256), :] - top)
            total = total + jnp.sum(e.reshape(32, 8, 256), axis=0)
            weighted = weighted + dot(vt[:, pl.ds(t * 256, 256)], e.astype(BF16))
        total = jnp.sum(total, axis=0, keepdims=True)
        otx[i] = weighted.astype(BF16)
        first = lax.broadcasted_iota(jnp.int32, (8, 256), 0) == 0
        sttx[i] = jnp.where(first, top, total)

        @pl.when(i > 0)
        def _():
            back = {"blk": source, "grp": g}
            remote(otx.at[i], orx.at[i], S_O + i, back).start()
            remote(sttx.at[i], strx.at[i], S_ST + i, back).start()

        return carry

    spread_wo(2)
    lax.fori_loop(0, 7, attend, 0)
    spread_wo(3)
    lax.fori_loop(7, 8, attend, 0)
    for i in range(1, 8):
        back = {"blk": blk_from(i), "grp": g}
        sent.append(remote(otx.at[i], orx.at[i], S_O + i, back))
        sent.append(remote(sttx.at[i], strx.at[i], S_ST + i, back))
    orx[0] = otx[0]
    strx[0] = sttx[0]
    for i in range(1, 8):
        arrived(orx.at[i], S_O + i)
        arrived(strx.at[i], S_ST + i)
    tops = [strx[i][0:1, :] for i in range(8)]
    top = functools.reduce(jnp.maximum, tops)
    total = jnp.zeros((1, 256), F32)
    weighted = jnp.zeros((HD, 256), F32)
    for i in range(8):
        factor = jnp.exp(tops[i] - top)
        total = total + factor * strx[i][1:2, :]
        weighted = weighted + orx[i].astype(F32) * factor
    mixed[0] = (weighted / total).T.astype(BF16)
    for load in self_loads:
        load.wait()
    spread_self(0)
    spread_wo(4)
    spread_wo(5)

    def project_and_sum(u, weight, between, finish):
        for h in range(2):
            def columns_of(i, carry):
                columns = pl.ds(pl.multiple_of(i * 512, 512), 512)
                y = dot(mixed[u], weight[i]).reshape(8, 2, 2, 8, 512)
                for cc in range(2):
                    part[u, cc, :, :, columns] = y[:, :, cc].reshape(8, 16, 512).astype(BF16)
                return carry

            lax.fori_loop(4 * h, 4 * h + 4, columns_of, 0)
            send(
                part.at[u, 1 - c, :, :, half_columns(h)], sib.at[u, :, :, half_columns(h)],
                S_RSC + 2 * u + h, sibling,
            )

        def chip_sum(zz, h):
            columns = half_columns(h)
            return part[u, c, zz, :, columns].astype(F32) + sib[u, zz, :, columns].astype(F32)

        def hop(k, way, h, start):
            if k == start and way == h:
                arrived(sib.at[u, :, :, half_columns(h)], S_RSC + 2 * u + h)
            zz = (z + k) % 8 if way == 0 else (z + 8 - k) % 8
            value = chip_sum(zz, h)
            at = S_RSZ + ((u * 2 + way) * 2 + h) * 5
            if k < start:
                arrived(rrx.at[u, way, h, k], at + k + 1)
                value = value + rrx[u, way, h, k].astype(F32)
            rtx[u, way, h, k - 1] = value.astype(BF16)
            send(rtx.at[u, way, h, k - 1], rrx.at[u, way, h, k - 1], at + k, vertical[way])

        for k in (4, 3, 2, 1):
            hop(k, 0, 0, 4)
            hop(k, 1, 1, 4)
            if k > 1:
                hop(k - 1, 0, 1, 3)
                hop(k - 1, 1, 0, 3)
            between(k)
        for h in range(2):
            value = chip_sum(z, h)
            for way in range(2):
                arrived(rrx.at[u, way, h, 0], S_RSZ + ((u * 2 + way) * 2 + h) * 5 + 1)
                value = value + rrx[u, way, h, 0].astype(F32)
            finish(h, value)

    def between_cross(k):
        if k == 2:
            spread_self(1)

    def finish_cross(h, value):
        columns = half_columns(h)
        carried16[:, columns] = latent16[:, columns] + value
        ztx[:, columns] = value.astype(BF16)
        send(ztx.at[:, columns], zrx.at[:, columns], S_RSY + h, across)

    project_and_sum(0, wo, between_cross, finish_cross)
    for h in range(2):
        arrived(zrx.at[:, half_columns(h)], S_RSY + h)
    spread_self(2)
    spread_so(0)
    carried = carried16[...] + zrx[...].astype(F32)
    own_carried = jnp.where(yh == 0, carried[:8], carried[8:])

    gather_begin(1, carried, gain_s[...])
    for k in range(1, 5):
        gather_step(1, k)
        if k == 2:
            spread_self(3)
        if k == 3:
            spread_so(1)
            spread_so(2)
    gather_end(1)
    spread_self(4)
    spread_self(5)

    qkv = natural(dot(latent_rows(1), sqkv[...].reshape(D, 3 * HD)), 3 * HD)
    queries = qkv[:, :HD].astype(BF16)
    kv2[b] = qkv[:, HD:].astype(BF16)

    def spread_keyval(stage):
        for n in range(4):
            spread(kv2, n * 64, 64, S_KV2 + 10 * n, n % 2 == 1, stage)

    def absorb(source, own):
        block = kv2[source]
        s = dot(block[:, :HD], queries, 1, 1) * SCALE
        if own:
            ids = lax.broadcasted_iota(jnp.int32, (256, 256), 0)
            s = jnp.where(ids <= lax.broadcasted_iota(jnp.int32, (256, 256), 1), s, LOW)
        top = jnp.max(s, axis=0, keepdims=True)
        if not own:
            top = jnp.maximum(top, top2[...])
        e = jnp.exp(s - top)
        total = jnp.sum(e, axis=0, keepdims=True)
        weighted = dot(block[:, HD:], e.astype(BF16), 0, 0)
        if not own:
            factor = jnp.exp(top2[...] - top)
            total = total + total2[...] * factor
            weighted = weighted + weighted2[...] * factor
        top2[...] = top
        total2[...] = total
        weighted2[...] = weighted

    def absorb_earlier(*slots):
        for i in slots:
            @pl.when(blk_from(i) < b)
            def _():
                absorb(blk_from(i), False)

    spread_keyval(0)
    spread_so(3)
    absorb(b, True)
    spread_keyval(1)
    spread_keyval(2)
    spread_keyval(3)
    spread_keyval(4)
    absorb_earlier(1, 3, 2)
    spread_keyval(5)
    absorb_earlier(4, 5, 7, 6)
    mixed[1] = (weighted2[...] / total2[...]).T.astype(BF16)

    spread_so(4)
    spread_so(5)
    def finish_self(h, value):
        columns = half_columns(h)
        out[:, columns] = own_carried[:, columns.start:columns.start + HALF] + jnp.where(yh == 0, value[:8], value[8:])
        ytx[:, columns] = jnp.where(yh == 0, value[8:], value[:8])
        send(ytx.at[:, columns], yrx.at[:, columns], S_RSY + 2 + h, across)

    project_and_sum(1, so, lambda k: None, finish_self)
    for h in range(2):
        columns = half_columns(h)
        arrived(yrx.at[:, columns], S_RSY + 2 + h)
        out[:, columns] = out[:, columns] + yrx[:, columns]

    for copy in sent:
        copy.wait_send()


def shards(*arguments):
    prefix, latent, limits, gain_p, gain_l, gain_s, *weights = arguments
    vmem = pl.BlockSpec(memory_space=pltpu.VMEM)
    sem = pltpu.SemaphoreType.DMA
    scratch = [
        ((6, 512, HD), BF16),
        ((2, HD, 512), BF16),
        ((1024, D), BF16),
        ((8, 512, 3 * HD), BF16),
        ((8, HD, 512), BF16),
        ((8, 512, 3 * HD), BF16),
        ((8, HD, 512), BF16),
        ((8, 8, 256), jnp.int32),
        ((8, 256, HD), BF16),
        ((1280, HD), BF16),
        ((HD, 1280), BF16),
        ((1024, 2 * HD), F32),
        ((1280, 256), F32),
        ((8, HD, 256), BF16),
        ((8, HD, 256), BF16),
        ((8, 8, 256), F32),
        ((8, 8, 256), F32),
        ((2, 256, HD), BF16),
        ((8, 256, 2 * HD), BF16),
        ((1, 256), F32),
        ((1, 256), F32),
        ((HD, 256), F32),
        ((16, HALF), BF16),
        ((16, HALF), BF16),
        ((2, 8, 2, 16, D), BF16),
        ((2, 2, 8, 16, D), BF16),
        ((2, 8, 16, D), BF16),
        ((2, 2, 2, 4, 16, HALF), BF16),
        ((2, 2, 2, 4, 16, HALF), BF16),
        ((8, D), F32),
        ((8, D), F32),
        ((16, D), BF16),
        ((16, D), BF16),
        ((16, D), F32),
        ((16, D), F32),
    ]
    return pl.pallas_call(
        layer_kernel,
        out_shape=jax.ShapeDtypeStruct((8, D), F32),
        in_specs=[pl.BlockSpec(memory_space=pl.ANY)] + [vmem] * 5
        + [pl.BlockSpec(memory_space=pl.ANY)] * 12,
        out_specs=vmem,
        scratch_shapes=[pltpu.VMEM(shape, dtype) for shape, dtype in scratch]
        + [sem((N_SEM,)), sem((N_SEM,)), sem((16,))],
        compiler_params=pltpu.CompilerParams(
            collective_id=0, has_side_effects=True, vmem_limit_bytes=56 * 1024 * 1024
        ),
        name="layer",
    )(
        prefix, latent, limits.reshape(1, -1),
        gain_p.reshape(1, -1), gain_l.reshape(1, -1), gain_s.reshape(1, -1), *weights,
    )


def solution(mesh):
    return jax.shard_map(
        shards,
        mesh=mesh,
        in_specs=(
            P("blk", None), P(("blk", "grp"), None), P("blk"), P(), P(), P(),
            P("blk", "grp"), P("blk", "grp"), P("blk", "grp"), P("grp", "blk"),
            P("blk", "grp"), P("blk", "grp"), P("blk", "grp"), P("grp", "blk"),
            P("blk", "grp"), P("blk", "grp"), P("blk", "grp"), P("grp", "blk"),
        ),
        out_specs=P(("blk", "grp"), None),
        check_vma=False,
    )
```

```python
import functools

import jax
import jax.numpy as jnp
from jax import lax
from jax.experimental import pallas as pl
from jax.experimental.pallas import tpu as pltpu
from jax.sharding import PartitionSpec as P

D = 4096
HD = 128
HALF = D // 2
EPS = 1e-05
SCALE = HD ** (-0.5)
LOW = -1e30
CLIP = -1e20
MESH = pl.DeviceIdType.MESH
F32 = jnp.float32
BF16 = jnp.bfloat16

N_SEM = 0


def _places(count):
    global N_SEM
    first = N_SEM
    N_SEM += count
    return first


S_W = _places(4 * 10)
S_WO = _places(10)
S_SQKV = _places(10)
S_SO = _places(10)
S_LIM = _places(8)
S_Q = _places(8)
S_O = _places(8)
S_ST = _places(8)
S_KV2 = _places(4 * 10)
S_AGY = _places(2)
S_AGZ = _places(2 * 2 * 5 * 2)
S_AGC = _places(2 * 8 * 2)
S_RSC = _places(4)
S_RSZ = _places(2 * 2 * 2 * 5)
S_RSY = _places(4)


def rms_rows(values, gain):
    inverse = lax.rsqrt(jnp.sum(values * values, axis=1, keepdims=True) * (1.0 / D) + EPS)
    return values * inverse * gain


def pack_rows(rows):
    half = rows.shape[1] // 2
    return jnp.concatenate([rows[:, :half], rows[:, half:]], axis=0)


def unpack_rows(packed):
    return jnp.concatenate([packed[:8], packed[8:]], axis=1)


def dot(a, b, ca=1, cb=0):
    return lax.dot_general(a, b, (((ca,), (cb,)), ((), ())), preferred_element_type=F32)


def layer_kernel(
    prefix, latent, limits, gain_p, gain_l, gain_s,
    cq, ck, cv, co, dq, dk, dv, do, sq, sk, sv, so_in,
    out,
    raw, raw_o, pre, wqkv, wo, sqkv, so, lim, qn, kn, vt, acc, scores,
    otx, orx, sttx, strx, mixed, kv2, top2, total2, weighted2,
    pk, pkr, gat, part, sib, rtx, rrx, ytx, yrx, ztx, zrx, latent16, carried16,
    ss, rs, ls,
):
    b = lax.axis_index("blk")
    g = lax.axis_index("grp")
    x, yl = b % 4, b // 4
    z, yh, c = g // 4, (g // 2) % 2, g % 2

    def blk_to(i):
        return {"blk": ((yl + i // 4) % 2) * 4 + (x + i % 4) % 4, "grp": g}

    def blk_from(i):
        return ((yl + i // 4) % 2) * 4 + (x + 4 - i % 4) % 4

    def grp_at(zz, yy, cc):
        return {"blk": b, "grp": (zz * 2 + yy) * 2 + cc}

    sibling = grp_at(z, yh, 1 - c)
    across = grp_at(z, 1 - yh, c)
    above = grp_at((z + 1) % 8, yh, c)
    below = grp_at((z + 7) % 8, yh, c)
    vertical = (above, below)

    def remote(src, dst, place, device):
        return pltpu.make_async_remote_copy(
            src_ref=src, dst_ref=dst, send_sem=ss.at[place], recv_sem=rs.at[place],
            device_id=device, device_id_type=MESH,
        )

    sent = []

    def send(src, dst, place, device):
        copy = remote(src, dst, place, device)
        copy.start()
        sent.append(copy)

    def arrived(dst, place):
        remote(dst, dst, place, sibling).wait_recv()

    barrier = pltpu.get_barrier_semaphore()
    for i in range(1, 8):
        pl.semaphore_signal(barrier, inc=1, device_id=blk_to(i), device_id_type=MESH)
    for device in (sibling, across, above, below):
        pl.semaphore_signal(barrier, inc=1, device_id=device, device_id_type=MESH)

    loads = [
        pltpu.make_async_copy(prefix.at[pl.ds(t * 256, 256)], pre.at[pl.ds(t * 256, 256)], ls.at[t])
        for t in range(4)
    ]
    raw_loads = [
        pltpu.make_async_copy(source, raw.at[n], ls.at[4 + n])
        for n, source in enumerate((cq, ck, cv, dq, dk, dv))
    ] + [
        pltpu.make_async_copy(source, raw_o.at[n], ls.at[10 + n]) for n, source in enumerate((co, do))
    ]
    self_loads = [
        pltpu.make_async_copy(source, sqkv.at[b, :, pl.ds(n * HD, HD)], ls.at[12 + n])
        for n, source in enumerate((sq, sk, sv))
    ] + [pltpu.make_async_copy(so_in, so.at[b], ls.at[15])]
    for load in raw_loads + self_loads:
        load.start()
    for load in loads:
        load.start()

    def perturbed(weight, delta):
        return (weight.astype(F32) + delta.astype(F32)).astype(BF16)

    rows_l = latent[...].astype(F32)
    pk[...] = pack_rows(rows_l).astype(BF16)
    lim[0] = jnp.broadcast_to(limits[...], (8, 256))
    for load in raw_loads:
        load.wait()
    for n in range(3):
        wqkv[b, :, n * HD:(n + 1) * HD] = perturbed(raw[n], raw[n + 3])
    pl.semaphore_wait(barrier, 11)

    right, left, beside = blk_to(1), blk_to(3), blk_to(4)

    def spread(buf, start, rows, place, y_first, stage):
        def here(i, piece=None):
            if piece is None:
                return buf.at[blk_from(i), pl.ds(start, rows)]
            return buf.at[blk_from(i), pl.ds(start + piece * (rows // 2), rows // 2)]

        if stage == 0:
            send(here(0), here(0), place + 4, beside)
            send(here(0), here(0), place + 1, right)
            send(here(0), here(0), place + 3, left)
        elif y_first and stage == 1:
            arrived(here(4), place + 4)
            send(here(4), here(4), place + 5, right)
            send(here(4), here(4), place + 7, left)
        elif y_first and stage == 2:
            arrived(here(1), place + 1)
            send(here(1, 0), here(1, 0), place + 2, right)
            arrived(here(3), place + 3)
            send(here(3, 1), here(3, 1), place + 8, left)
        elif y_first and stage == 3:
            arrived(here(5), place + 5)
            send(here(5, 0), here(5, 0), place + 6, right)
            arrived(here(7), place + 7)
            send(here(7, 1), here(7, 1), place + 9, left)
        elif y_first and stage == 4:
            arrived(here(2, 0), place + 2)
            arrived(here(2, 1), place + 8)
        elif y_first:
            arrived(here(6, 0), place + 6)
            arrived(here(6, 1), place + 9)
        elif stage == 1:
            arrived(here(1), place + 1)
            send(here(1, 0), here(1, 0), place + 2, right)
            send(here(1), here(1), place + 5, beside)
            arrived(here(3), place + 3)
            send(here(3, 1), here(3, 1), place + 8, left)
            send(here(3), here(3), place + 7, beside)
        elif stage == 2:
            arrived(here(2, 0), place + 2)
            arrived(here(2, 1), place + 8)
            send(here(2), here(2), place + 6, beside)
        elif stage == 5:
            for i in (4, 5, 7, 6):
                arrived(here(i), place + i)

    def spread_cross(stage, parts):
        for n in parts:
            start, rows = ((0, 96), (96, 160), (256, 128), (384, 128))[n]
            spread(wqkv, start, rows, S_W + 10 * n, n % 2 == 1, stage)

    def spread_self(stage):
        spread(sqkv, 0, 512, S_SQKV, True, stage)

    def spread_wo(stage):
        spread(wo, 0, HD, S_WO, True, stage)

    def spread_so(stage):
        spread(so, 0, HD, S_SO, True, stage)

    def own_and_other(own, other):
        return jnp.concatenate([jnp.where(yh == 0, own, other), jnp.where(yh == 0, other, own)], axis=0)

    def half_columns(h):
        return pl.ds(h * HALF, HALF)

    def gather_begin(u, rows, gain):
        gat[u, z, c] = rms_rows(rows, gain).astype(BF16)
        for n in range(2):
            for way in range(2):
                h = n if way == 0 else 1 - n
                own = gat.at[u, z, c, :, half_columns(h)]
                send(own, own, S_AGZ + ((u * 2 + way) * 5 + 1) * 2 + h, vertical[way])
        for h in range(2):
            own = gat.at[u, z, c, :, half_columns(h)]
            send(own, own, S_AGC + u * 16 + h, sibling)

    def gather_step(u, k):
        for n in range(2):
            for way in range(2):
                h = n if way == 0 else 1 - n
                if k == 4 and n == 1:
                    continue
                zz = (z + 8 - k) % 8 if way == 0 else (z + k) % 8
                chunk = gat.at[u, zz, c, :, half_columns(h)]
                arrived(chunk, S_AGZ + ((u * 2 + way) * 5 + k) * 2 + h)
                if k < 3 or k == 3 and n == 0:
                    send(chunk, chunk, S_AGZ + ((u * 2 + way) * 5 + k + 1) * 2 + h, vertical[way])
                send(chunk, chunk, S_AGC + u * 16 + (k if way == 0 else 8 - k) * 2 + h, sibling)

    def gather_end(u, places):
        for k in places:
            for h in range(2):
                arrived(gat.at[u, (z + 8 - k) % 8, 1 - c, :, half_columns(h)], S_AGC + u * 16 + 2 * k + h)

    send(pk, pkr, S_AGY, across)
    spread_cross(0, (0, 1, 2, 3))
    for i in range(1, 8):
        send(lim.at[0], lim.at[i], S_LIM + i, blk_to(i))

    def norm_prefix(t):
        if t % 2 == 0:
            loads[t // 2].wait()

        def tile(n, carry):
            rows = pl.ds(pl.multiple_of(t * 128 + n * 16, 16), 16)
            pre[rows, :] = rms_rows(pre[rows, :].astype(F32), gain_p[...]).astype(BF16)
            return carry

        lax.fori_loop(0, 8, tile, 0)

    def prefix_part(row, first):
        columns = pl.ds(pl.multiple_of(row * HALF, HALF), HALF)
        weights = wqkv[pl.ds(row * 4, 4), :, HD:].reshape(HALF, 2 * HD)
        for t in range(2):
            rows = pl.ds(t * 512, 512)
            piece = dot(pre[rows, columns], weights)
            acc[rows, :] = piece if first else acc[rows, :] + piece

    def latent_rows(u):
        return gat[u].reshape(256, D)

    def natural(values, width):
        cut = values.reshape(-1, 2, 2, 8, width)
        order = jnp.stack([cut[:, cc, yy] for yy in range(2) for cc in range(2)], axis=1)
        return order.reshape(values.shape[0], width)

    norm_prefix(0)
    arrived(pkr, S_AGY)
    latent16[...] = own_and_other(rows_l, unpack_rows(pkr[...].astype(F32)))
    gather_begin(0, latent16[...], gain_l[...])
    norm_prefix(1)
    spread_cross(1, (0, 1))
    gather_step(0, 1)
    norm_prefix(2)
    gather_step(0, 2)
    spread_cross(1, (2, 3))
    norm_prefix(3)
    spread_cross(2, (0, 1))
    norm_prefix(4)
    gather_step(0, 3)
    spread_cross(2, (2, 3))
    norm_prefix(5)
    spread_cross(3, (0, 1))
    gather_step(0, 4)
    norm_prefix(6)
    spread_cross(3, (2, 3))
    norm_prefix(7)
    wo[b] = perturbed(raw_o[0], raw_o[1])
    spread_wo(0)
    spread_cross(4, (0, 1, 2, 3))
    prefix_part(yl, True)
    gather_end(0, range(8))
    spread_cross(5, (0, 1, 2, 3))
    qn[0] = natural(dot(latent_rows(0), wqkv[:, :, :HD].reshape(D, HD)), HD).astype(BF16)
    for i in (4, 5, 7, 6, 1, 3, 2):
        send(qn.at[0], qn.at[i], S_Q + i, blk_to(i))
    spread_wo(1)
    prefix_part(1 - yl, False)
    latent_kv = natural(dot(latent_rows(0), wqkv[:, :, HD:].reshape(D, 2 * HD)), 2 * HD)
    for t in range(5):
        rows = pl.ds(t * 256, 256)
        values = acc[rows, :] if t < 4 else latent_kv
        kn[rows, :] = values[:, :HD].astype(BF16)
        vt[:, rows] = values[:, HD:].T.astype(BF16)

    def attend(i):
        source = blk_from(i)
        queries = qn[i]
        seen = lim[i][0:1, :]
        high = jnp.full((8, 256), CLIP, F32)
        for t in range(5):
            s = dot(kn[pl.ds(t * 256, 256), :], queries, 1, 1) * SCALE
            ids = lax.broadcasted_iota(jnp.int32, (256, 256), 0)
            if t < 4:
                allowed = ids + (b * 1024 + t * 256) < seen
            else:
                allowed = ids + b * 256 <= lax.broadcasted_iota(jnp.int32, (256, 256), 1) + source * 256
            s = jnp.where(allowed, s, LOW)
            scores[pl.ds(t * 256, 256), :] = s
            high = jnp.maximum(high, jnp.max(s.reshape(32, 8, 256), axis=0))
        top = jnp.max(high, axis=0, keepdims=True)
        total = jnp.zeros((8, 256), F32)
        weighted = jnp.zeros((HD, 256), F32)
        for t in range(5):
            e = jnp.exp(scores[pl.ds(t * 256, 256), :] - top)
            total = total + jnp.sum(e.reshape(32, 8, 256), axis=0)
            weighted = weighted + dot(vt[:, pl.ds(t * 256, 256)], e.astype(BF16))
        return top, jnp.sum(total, axis=0, keepdims=True), weighted

    def keep(i, top, total, weighted):
        otx[i] = weighted.astype(BF16)
        first = lax.broadcasted_iota(jnp.int32, (2, 256), 0) == 0
        sttx[i] = jnp.where(first, top, total)

    def across_copies(i):
        return (
            remote(otx.at[i], orx.at[i], S_O + i, beside),
            remote(sttx.at[i], strx.at[i], S_ST + i, beside),
        )

    def along_copies(i):
        back = {"blk": blk_from(i), "grp": g}
        return (
            remote(otx.at[i], orx.at[i], S_O + i, back),
            remote(sttx.at[i], strx.at[i], S_ST + i, back),
        )

    def attend_partner_row(n, carry):
        i = n + 4
        arrived(lim.at[i], S_LIM + i)
        arrived(qn.at[i], S_Q + i)
        keep(i, *attend(i))
        for copy in across_copies(i):
            copy.start()
        return carry

    def attend_own_row(n, carry):
        i = (n + 1) % 4

        @pl.when(i > 0)
        def _():
            arrived(lim.at[i], S_LIM + i)
            arrived(qn.at[i], S_Q + i)

        top, total, weighted = attend(i)
        arrived(orx.at[i + 4], S_O + i + 4)
        arrived(strx.at[i + 4], S_ST + i + 4)
        top_there = strx[i + 4][0:1, :]
        both = jnp.maximum(top, top_there)
        here_part, there_part = jnp.exp(top - both), jnp.exp(top_there - both)
        keep(
            i, both, total * here_part + strx[i + 4][1:2, :] * there_part,
            weighted * here_part + orx[i + 4].astype(F32) * there_part,
        )

        @pl.when(i > 0)
        def _():
            for copy in along_copies(i):
                copy.start()

        return carry

    spread_wo(2)
    lax.fori_loop(0, 4, attend_partner_row, 0)
    lax.fori_loop(0, 3, attend_own_row, 0)
    spread_wo(3)
    lax.fori_loop(3, 4, attend_own_row, 0)
    for i in range(1, 8):
        sent.extend(along_copies(i) if i < 4 else across_copies(i))

    orx[0] = otx[0]
    strx[0] = sttx[0]
    for i in range(1, 4):
        arrived(orx.at[i], S_O + i)
        arrived(strx.at[i], S_ST + i)
    tops = [strx[i][0:1, :] for i in range(4)]
    top = functools.reduce(jnp.maximum, tops)
    total = jnp.zeros((1, 256), F32)
    weighted = jnp.zeros((HD, 256), F32)
    for i in range(4):
        factor = jnp.exp(tops[i] - top)
        total = total + factor * strx[i][1:2, :]
        weighted = weighted + orx[i].astype(F32) * factor
    mixed[0] = (weighted / total).T.astype(BF16)
    for load in self_loads:
        load.wait()
    spread_self(0)
    spread_wo(4)
    spread_wo(5)

    def project_and_sum(u, weight, between, finish):
        for h in range(2):
            def columns_of(i, carry):
                columns = pl.ds(pl.multiple_of(i * 512, 512), 512)
                y = dot(mixed[u], weight[i]).reshape(8, 2, 2, 8, 512)
                for cc in range(2):
                    part[u, cc, :, :, columns] = y[:, :, cc].reshape(8, 16, 512).astype(BF16)
                return carry

            lax.fori_loop(4 * h, 4 * h + 4, columns_of, 0)
            send(
                part.at[u, 1 - c, :, :, half_columns(h)], sib.at[u, :, :, half_columns(h)],
                S_RSC + 2 * u + h, sibling,
            )

        def chip_sum(zz, h):
            columns = half_columns(h)
            return part[u, c, zz, :, columns].astype(F32) + sib[u, zz, :, columns].astype(F32)

        def hop(k, way, h, start):
            if k == start and way == h:
                arrived(sib.at[u, :, :, half_columns(h)], S_RSC + 2 * u + h)
            zz = (z + k) % 8 if way == 0 else (z + 8 - k) % 8
            value = chip_sum(zz, h)
            at = S_RSZ + ((u * 2 + way) * 2 + h) * 5
            if k < start:
                arrived(rrx.at[u, way, h, k], at + k + 1)
                value = value + rrx[u, way, h, k].astype(F32)
            rtx[u, way, h, k - 1] = value.astype(BF16)
            send(rtx.at[u, way, h, k - 1], rrx.at[u, way, h, k - 1], at + k, vertical[way])

        for k in (4, 3, 2, 1):
            hop(k, 0, 0, 4)
            hop(k, 1, 1, 4)
            if k > 1:
                hop(k - 1, 0, 1, 3)
                hop(k - 1, 1, 0, 3)
            between(k)
        for h in range(2):
            value = chip_sum(z, h)
            for way in range(2):
                arrived(rrx.at[u, way, h, 0], S_RSZ + ((u * 2 + way) * 2 + h) * 5 + 1)
                value = value + rrx[u, way, h, 0].astype(F32)
            finish(h, value)

    def between_cross(k):
        if k == 3:
            spread_self(1)
        if k == 1:
            spread_self(2)

    def finish_cross(h, value):
        columns = half_columns(h)
        carried16[:, columns] = latent16[:, columns] + value
        ztx[:, columns] = value.astype(BF16)
        send(ztx.at[:, columns], zrx.at[:, columns], S_RSY + h, across)

    project_and_sum(0, wo, between_cross, finish_cross)
    for h in range(2):
        arrived(zrx.at[:, half_columns(h)], S_RSY + h)
    carried = carried16[...] + zrx[...].astype(F32)
    own_carried = jnp.where(yh == 0, carried[:8], carried[8:])

    gather_begin(1, carried, gain_s[...])
    spread_self(3)
    spread_so(0)

    def arrived_rows(places):
        return jnp.concatenate([gat[1, (z + 8 - k) % 8].reshape(32, D) for k in places], axis=0)

    def keyval(places, start):
        rows = natural(dot(arrived_rows(places), sqkv[:, :, HD:].reshape(D, 2 * HD)), 2 * HD)
        kv2[b, pl.ds(start, 32 * len(places))] = rows.astype(BF16)

    def spread_keyval(stage, parts):
        for n in parts:
            start, rows = ((0, 64), (64, 96), (160, 32), (192, 64))[n]
            spread(kv2, start, rows, S_KV2 + 10 * n, n % 2 == 1, stage)

    near, far = (0, 1, 7, 2, 6), (3, 5, 4)
    gather_step(1, 1)
    gather_step(1, 2)
    spread_so(1)
    gather_step(1, 3)
    spread_self(4)
    spread_self(5)
    gather_end(1, near)
    keyval(near, 0)
    spread_keyval(0, (0, 1))
    gather_step(1, 4)
    gather_end(1, far)
    keyval(far, 160)
    spread_keyval(0, (2, 3))
    spread_keyval(1, (0, 1))
    spread_so(2)
    queries = natural(dot(latent_rows(1), sqkv[:, :, :HD].reshape(D, HD)), HD).astype(BF16)

    def absorb(source, own):
        block = kv2[source]
        s = dot(block[:, :HD], queries, 1, 1) * SCALE
        if own:
            row = lax.broadcasted_iota(jnp.int32, (256, 256), 0)
            place = row >> 5
            distance = (place + 1) >> 1
            ids = ((z + 8 + jnp.where((place & 1) == 1, -distance, distance)) & 7) * 32 + (row & 31)
            s = jnp.where(ids <= lax.broadcasted_iota(jnp.int32, (256, 256), 1), s, LOW)
        top = jnp.max(s, axis=0, keepdims=True)
        if not own:
            top = jnp.maximum(top, top2[...])
        e = jnp.exp(s - top)
        total = jnp.sum(e, axis=0, keepdims=True)
        weighted = dot(block[:, HD:], e.astype(BF16), 0, 0)
        if not own:
            factor = jnp.exp(top2[...] - top)
            total = total + total2[...] * factor
            weighted = weighted + weighted2[...] * factor
        top2[...] = top
        total2[...] = total
        weighted2[...] = weighted

    def absorb_earlier(*slots):
        for i in slots:
            @pl.when(blk_from(i) < b)
            def _():
                absorb(blk_from(i), False)

    absorb(b, True)
    spread_keyval(2, (0, 1))
    spread_keyval(1, (2, 3))
    spread_keyval(3, (0, 1))
    spread_keyval(2, (2, 3))
    spread_so(3)
    spread_keyval(3, (2, 3))
    spread_keyval(4, range(4))
    absorb_earlier(1, 3, 2)
    spread_keyval(5, range(4))
    absorb_earlier(4, 5, 7, 6)
    mixed[1] = (weighted2[...] / total2[...]).T.astype(BF16)

    spread_so(4)
    spread_so(5)
    def finish_self(h, value):
        columns = half_columns(h)
        out[:, columns] = own_carried[:, columns.start:columns.start + HALF] + jnp.where(yh == 0, value[:8], value[8:])
        ytx[h] = pack_rows(jnp.where(yh == 0, value[8:], value[:8])).astype(BF16)
        send(ytx.at[h], yrx.at[h], S_RSY + 2 + h, across)

    project_and_sum(1, so, lambda k: None, finish_self)
    for h in range(2):
        columns = half_columns(h)
        arrived(yrx.at[h], S_RSY + 2 + h)
        out[:, columns] = out[:, columns] + unpack_rows(yrx[h].astype(F32))

    for copy in sent:
        copy.wait_send()


def shards(*arguments):
    prefix, latent, limits, gain_p, gain_l, gain_s, *weights = arguments
    vmem = pl.BlockSpec(memory_space=pltpu.VMEM)
    sem = pltpu.SemaphoreType.DMA
    scratch = [
        ((6, 512, HD), BF16),
        ((2, HD, 512), BF16),
        ((1024, D), BF16),
        ((8, 512, 3 * HD), BF16),
        ((8, HD, 512), BF16),
        ((8, 512, 3 * HD), BF16),
        ((8, HD, 512), BF16),
        ((8, 8, 256), jnp.int32),
        ((8, 256, HD), BF16),
        ((1280, HD), BF16),
        ((HD, 1280), BF16),
        ((1024, 2 * HD), F32),
        ((1280, 256), F32),
        ((8, HD, 256), BF16),
        ((8, HD, 256), BF16),
        ((8, 2, 256), F32),
        ((8, 2, 256), F32),
        ((2, 256, HD), BF16),
        ((8, 256, 2 * HD), BF16),
        ((1, 256), F32),
        ((1, 256), F32),
        ((HD, 256), F32),
        ((16, HALF), BF16),
        ((16, HALF), BF16),
        ((2, 8, 2, 16, D), BF16),
        ((2, 2, 8, 16, D), BF16),
        ((2, 8, 16, D), BF16),
        ((2, 2, 2, 4, 16, HALF), BF16),
        ((2, 2, 2, 4, 16, HALF), BF16),
        ((2, 16, HALF // 2), BF16),
        ((2, 16, HALF // 2), BF16),
        ((16, D), BF16),
        ((16, D), BF16),
        ((16, D), F32),
        ((16, D), F32),
    ]
    return pl.pallas_call(
        layer_kernel,
        out_shape=jax.ShapeDtypeStruct((8, D), F32),
        in_specs=[pl.BlockSpec(memory_space=pl.ANY)] + [vmem] * 5
        + [pl.BlockSpec(memory_space=pl.ANY)] * 12,
        out_specs=vmem,
        scratch_shapes=[pltpu.VMEM(shape, dtype) for shape, dtype in scratch]
        + [sem((N_SEM,)), sem((N_SEM,)), sem((16,))],
        compiler_params=pltpu.CompilerParams(
            collective_id=0, has_side_effects=True, vmem_limit_bytes=56 * 1024 * 1024
        ),
        name="layer",
    )(
        prefix, latent, limits.reshape(1, -1),
        gain_p.reshape(1, -1), gain_l.reshape(1, -1), gain_s.reshape(1, -1), *weights,
    )


def solution(mesh):
    return jax.shard_map(
        shards,
        mesh=mesh,
        in_specs=(
            P("blk", None), P(("blk", "grp"), None), P("blk"), P(), P(), P(),
            P("blk", "grp"), P("blk", "grp"), P("blk", "grp"), P("grp", "blk"),
            P("blk", "grp"), P("blk", "grp"), P("blk", "grp"), P("grp", "blk"),
            P("blk", "grp"), P("blk", "grp"), P("blk", "grp"), P("grp", "blk"),
        ),
        out_specs=P(("blk", "grp"), None),
        check_vma=False,
    )
```

```python
import functools
import math

import jax
import jax.numpy as jnp
from jax import lax
from jax.experimental import pallas as pl
from jax.experimental.pallas import tpu as pltpu
from jax.sharding import PartitionSpec as P

D = 4096
HD = 128
HALF = D // 2
EPS = 1e-05
SCALE = HD ** (-0.5)
LOW = -1e30
CLIP = -1e20
MESH = pl.DeviceIdType.MESH
F32 = jnp.float32
BF16 = jnp.bfloat16

N_SEM = 0


def _places(count):
    global N_SEM
    first = N_SEM
    N_SEM += count
    return first


S_W = _places(4 * 7) - 1
S_WO = _places(7) - 1
S_SQKV = _places(7) - 1
S_SO = _places(7) - 1
S_LIM = _places(1)
S_Q = _places(7) - 1
S_O = _places(7) - 1
S_ST = _places(7) - 1
S_KV2 = _places(4 * 7) - 1
S_AGY = _places(1)
S_AGZ = _places(2 * 2 * 7)
S_AGC = _places(3)
S_RSC = _places(4)
S_RSZ = _places(2 * 2 * 2 * 4) - 1
S_RSY = _places(4)

GROUP_KIB = 1100
N_GROUPS = 18


def rms_rows(values, gain):
    inverse = lax.rsqrt(jnp.sum(values * values, axis=1, keepdims=True) * (1.0 / D) + EPS)
    return values * inverse * gain


def pack_rows(rows):
    half = rows.shape[1] // 2
    return jnp.concatenate([rows[:, :half], rows[:, half:]], axis=0)


def unpack_rows(packed):
    return jnp.concatenate([packed[:8], packed[8:]], axis=1)


def dot(a, b, ca=1, cb=0):
    return lax.dot_general(a, b, (((ca,), (cb,)), ((), ())), preferred_element_type=F32)


def layer_kernel(
    prefix, latent, limits, gain_p, gain_l, gain_s,
    cq, ck, cv, co, dq, dk, dv, do, sq, sk, sv, so_in,
    out,
    raw, raw_o, pre, wqkv, wo, sqkv, so, lim, qn, kn, vt, acc, scores,
    otx, orx, sttx, strx, mixed, kv2, top2, total2, weighted2,
    pk, pkr, gat, part, sib, rtx, rrx, ytx, yrx, ztx, zrx, latent16, carried16,
    ss, rs, ls,
):
    b = lax.axis_index("blk")
    g = lax.axis_index("grp")
    x, yl = b % 4, b // 4
    z, yh, c = g // 4, (g // 2) % 2, g % 2

    def blk_to(i):
        return {"blk": ((yl + i // 4) % 2) * 4 + (x + i % 4) % 4, "grp": g}

    def blk_from(i):
        return ((yl + i // 4) % 2) * 4 + (x + 4 - i % 4) % 4

    def grp_at(zz, yy, cc):
        return {"blk": b, "grp": (zz * 2 + yy) * 2 + cc}

    sibling = grp_at(z, yh, 1 - c)
    across = grp_at(z, 1 - yh, c)
    above = grp_at((z + 1) % 8, yh, c)
    below = grp_at((z + 7) % 8, yh, c)
    vertical = (above, below)

    def remote(src, dst, place, device, group=0):
        return pltpu.make_async_remote_copy(
            src_ref=src, dst_ref=dst, send_sem=ss.at[group], recv_sem=rs.at[place],
            device_id=device, device_id_type=MESH,
        )

    sent_kib = [0]

    def group_for(src, count=1):
        kib = count * math.prod(src.shape) * jnp.dtype(src.dtype).itemsize // 1024
        if sent_kib[-1] + kib > GROUP_KIB and sent_kib[-1] % 8 == 0:
            sent_kib.append(0)
        sent_kib[-1] += kib
        return len(sent_kib) - 1

    def send(src, dst, place, device):
        remote(src, dst, place, device, group_for(src)).start()

    def arrived(dst, place):
        remote(dst, dst, place, sibling).wait_recv()

    barrier = pltpu.get_barrier_semaphore()
    for i in range(1, 8):
        pl.semaphore_signal(barrier, inc=1, device_id=blk_to(i), device_id_type=MESH)
    for device in (sibling, across, above, below):
        pl.semaphore_signal(barrier, inc=1, device_id=device, device_id_type=MESH)

    loads = [
        pltpu.make_async_copy(prefix.at[pl.ds(t * 256, 256)], pre.at[pl.ds(t * 256, 256)], ls.at[t])
        for t in range(4)
    ]
    raw_loads = [
        pltpu.make_async_copy(source, raw.at[n], ls.at[4]) for n, source in enumerate((cq, ck, cv, dq, dk, dv))
    ] + [
        pltpu.make_async_copy(source, raw_o.at[n], ls.at[5]) for n, source in enumerate((co, do))
    ]
    self_loads = [
        pltpu.make_async_copy(source, sqkv.at[b, :, pl.ds(n * HD, HD)], ls.at[6])
        for n, source in enumerate((sq, sk, sv))
    ] + [pltpu.make_async_copy(so_in, so.at[b], ls.at[7])]
    for load in raw_loads + self_loads:
        load.start()
    for load in loads:
        load.start()

    def perturbed(weight, delta):
        return (weight.astype(F32) + delta.astype(F32)).astype(BF16)

    rows_l = latent[...].astype(F32)
    pk[...] = pack_rows(rows_l).astype(BF16)
    lim[0] = jnp.broadcast_to(limits[...], (8, 256))
    pltpu.make_async_copy(raw, raw, ls.at[4]).wait()
    for n in range(3):
        wqkv[b, :, n * HD:(n + 1) * HD] = perturbed(raw[n], raw[n + 3])
    pl.semaphore_wait(barrier, 11)

    right, left, beside = blk_to(1), blk_to(3), blk_to(4)

    def spread(buf, start, rows, place, y_first, stage):
        def here(i, piece=None):
            if piece is None:
                return buf.at[blk_from(i), pl.ds(start, rows)]
            return buf.at[blk_from(i), pl.ds(start + piece * (rows // 2), rows // 2)]

        if stage == 0:
            send(here(0), here(0), place + 4, beside)
            send(here(0), here(0), place + 1, right)
            send(here(0), here(0), place + 3, left)
        elif y_first and stage == 1:
            arrived(here(4), place + 4)
            send(here(4), here(4), place + 5, right)
            send(here(4), here(4), place + 7, left)
        elif y_first and stage == 2:
            arrived(here(1), place + 1)
            send(here(1, 0), here(1, 0), place + 2, right)
            arrived(here(3), place + 3)
            send(here(3, 1), here(3, 1), place + 2, left)
        elif y_first and stage == 3:
            arrived(here(5), place + 5)
            send(here(5, 0), here(5, 0), place + 6, right)
            arrived(here(7), place + 7)
            send(here(7, 1), here(7, 1), place + 6, left)
        elif y_first and stage == 4:
            arrived(here(2), place + 2)
        elif y_first:
            arrived(here(6), place + 6)
        elif stage == 1:
            arrived(here(1), place + 1)
            send(here(1, 0), here(1, 0), place + 2, right)
            send(here(1), here(1), place + 5, beside)
            arrived(here(3), place + 3)
            send(here(3, 1), here(3, 1), place + 2, left)
            send(here(3), here(3), place + 7, beside)
        elif stage == 2:
            arrived(here(2), place + 2)
            send(here(2), here(2), place + 6, beside)
        elif stage == 5:
            for i in (4, 5, 7, 6):
                arrived(here(i), place + i)

    def spread_cross(stage, parts):
        for n in parts:
            start, rows = ((0, 96), (96, 160), (256, 128), (384, 128))[n]
            spread(wqkv, start, rows, S_W + 7 * n, n % 2 == 1, stage)

    def spread_self(stage):
        spread(sqkv, 0, 512, S_SQKV, True, stage)

    def spread_wo(stage):
        spread(wo, 0, HD, S_WO, True, stage)

    def spread_so(stage):
        spread(so, 0, HD, S_SO, True, stage)

    def own_and_other(own, other):
        return jnp.concatenate([jnp.where(yh == 0, own, other), jnp.where(yh == 0, other, own)], axis=0)

    def half_columns(h):
        return pl.ds(h * HALF, HALF)

    def agz(u, way, k, h):
        return S_AGZ + (u * 2 + way) * 7 + (k - 1) * 2 + (h if k < 4 else 0)

    def agc(u, place):
        return S_AGC + (u if place not in (3, 4, 5) else 2 * u)

    def gather_begin(u, rows, gain):
        gat[u, z, c] = rms_rows(rows, gain).astype(BF16)
        for n in range(2):
            for way in range(2):
                h = n if way == 0 else 1 - n
                own = gat.at[u, z, c, :, half_columns(h)]
                send(own, own, agz(u, way, 1, h), vertical[way])
        for h in range(2):
            own = gat.at[u, z, c, :, half_columns(h)]
            send(own, own, agc(u, 0), sibling)

    def gather_step(u, k):
        for n in range(2):
            for way in range(2):
                h = n if way == 0 else 1 - n
                if k == 4 and n == 1:
                    continue
                zz = (z + 8 - k) % 8 if way == 0 else (z + k) % 8
                chunk = gat.at[u, zz, c, :, half_columns(h)]
                arrived(chunk, agz(u, way, k, h))
                if k < 3 or k == 3 and n == 0:
                    send(chunk, chunk, agz(u, way, k + 1, h), vertical[way])
                send(chunk, chunk, agc(u, k if way == 0 else 8 - k), sibling)

    def gather_end(u, places):
        arrived(gat.at[u, pl.ds(0, len(places)), 1 - c], agc(u, places[0]))

    send(pk, pkr, S_AGY, across)
    spread_cross(0, (0, 1, 2, 3))
    for i in range(1, 8):
        send(lim.at[0], lim.at[i], S_LIM, blk_to(i))

    def norm_prefix(t):
        if t % 2 == 0:
            loads[t // 2].wait()

        def tile(n, carry):
            rows = pl.ds(pl.multiple_of(t * 128 + n * 16, 16), 16)
            pre[rows, :] = rms_rows(pre[rows, :].astype(F32), gain_p[...]).astype(BF16)
            return carry

        lax.fori_loop(0, 8, tile, 0)

    def prefix_part(row, first):
        columns = pl.ds(pl.multiple_of(row * HALF, HALF), HALF)
        weights = wqkv[pl.ds(row * 4, 4), :, HD:].reshape(HALF, 2 * HD)
        for t in range(2):
            rows = pl.ds(t * 512, 512)
            piece = dot(pre[rows, columns], weights)
            acc[rows, :] = piece if first else acc[rows, :] + piece

    def latent_rows(u):
        return gat[u].reshape(256, D)

    def natural(values, width):
        cut = values.reshape(-1, 2, 2, 8, width)
        order = jnp.stack([cut[:, cc, yy] for yy in range(2) for cc in range(2)], axis=1)
        return order.reshape(values.shape[0], width)

    norm_prefix(0)
    arrived(pkr, S_AGY)
    latent16[...] = own_and_other(rows_l, unpack_rows(pkr[...].astype(F32)))
    gather_begin(0, latent16[...], gain_l[...])
    norm_prefix(1)
    spread_cross(1, (0, 1))
    gather_step(0, 1)
    norm_prefix(2)
    gather_step(0, 2)
    spread_cross(1, (2, 3))
    norm_prefix(3)
    spread_cross(2, (0, 1))
    norm_prefix(4)
    gather_step(0, 3)
    spread_cross(2, (2, 3))
    norm_prefix(5)
    spread_cross(3, (0, 1))
    gather_step(0, 4)
    norm_prefix(6)
    spread_cross(3, (2, 3))
    norm_prefix(7)
    pltpu.make_async_copy(raw_o, raw_o, ls.at[5]).wait()
    wo[b] = perturbed(raw_o[0], raw_o[1])
    spread_wo(0)
    spread_cross(4, (0, 1, 2, 3))
    prefix_part(yl, True)
    gather_end(0, range(8))
    spread_cross(5, (0, 1, 2, 3))
    qn[0] = natural(dot(latent_rows(0), wqkv[:, :, :HD].reshape(D, HD)), HD).astype(BF16)
    for i in (4, 5, 7, 6, 1, 3, 2):
        send(qn.at[0], qn.at[i], S_Q + i, blk_to(i))
    prefix_part(1 - yl, False)
    spread_wo(1)
    latent_kv = natural(dot(latent_rows(0), wqkv[:, :, HD:].reshape(D, 2 * HD)), 2 * HD)
    for t in range(5):
        rows = pl.ds(t * 256, 256)
        values = acc[rows, :] if t < 4 else latent_kv
        kn[rows, :] = values[:, :HD].astype(BF16)
        vt[:, rows] = values[:, HD:].T.astype(BF16)

    def attend(i):
        source = blk_from(i)
        queries = qn[i]
        seen = lim[i][0:1, :]
        high = jnp.full((8, 256), CLIP, F32)
        for t in range(5):
            s = dot(kn[pl.ds(t * 256, 256), :], queries, 1, 1) * SCALE
            ids = lax.broadcasted_iota(jnp.int32, (256, 256), 0)
            if t < 4:
                allowed = ids + (b * 1024 + t * 256) < seen
            else:
                allowed = ids + b * 256 <= lax.broadcasted_iota(jnp.int32, (256, 256), 1) + source * 256
            s = jnp.where(allowed, s, LOW)
            scores[pl.ds(t * 256, 256), :] = s
            high = jnp.maximum(high, jnp.max(s.reshape(32, 8, 256), axis=0))
        top = jnp.max(high, axis=0, keepdims=True)
        total = jnp.zeros((8, 256), F32)
        weighted = jnp.zeros((HD, 256), F32)
        for t in range(5):
            e = jnp.exp(scores[pl.ds(t * 256, 256), :] - top)
            total = total + jnp.sum(e.reshape(32, 8, 256), axis=0)
            weighted = weighted + dot(vt[:, pl.ds(t * 256, 256)], e.astype(BF16))
        return top, jnp.sum(total, axis=0, keepdims=True), weighted

    def keep(i, top, total, weighted):
        otx[i] = weighted.astype(BF16)
        first = lax.broadcasted_iota(jnp.int32, (2, 256), 0) == 0
        sttx[i] = jnp.where(first, top, total)

    output_group = group_for(otx.at[0], 7)

    def across_copies(i):
        return (
            remote(otx.at[i], orx.at[i], S_O + i, beside, output_group),
            remote(sttx.at[i], strx.at[i], S_ST + i, beside, N_GROUPS - 1),
        )

    def along_copies(i):
        back = {"blk": blk_from(i), "grp": g}
        return (
            remote(otx.at[i], orx.at[i], S_O + i, back, output_group),
            remote(sttx.at[i], strx.at[i], S_ST + i, back, N_GROUPS - 1),
        )

    def attend_partner_row(n, carry):
        i = n + 4
        arrived(qn.at[i], S_Q + i)
        keep(i, *attend(i))
        for copy in across_copies(i):
            copy.start()
        return carry

    def attend_own_row(n, carry):
        i = (n + 1) % 4

        @pl.when(i > 0)
        def _():
            arrived(qn.at[i], S_Q + i)

        top, total, weighted = attend(i)
        arrived(orx.at[i + 4], S_O + i + 4)
        arrived(strx.at[i + 4], S_ST + i + 4)
        top_there = strx[i + 4][0:1, :]
        both = jnp.maximum(top, top_there)
        here_part, there_part = jnp.exp(top - both), jnp.exp(top_there - both)
        keep(
            i, both, total * here_part + strx[i + 4][1:2, :] * there_part,
            weighted * here_part + orx[i + 4].astype(F32) * there_part,
        )

        @pl.when(i > 0)
        def _():
            for copy in along_copies(i):
                copy.start()

        return carry

    spread_wo(2)
    arrived(lim.at[pl.ds(1, 7)], S_LIM)
    lax.fori_loop(0, 4, attend_partner_row, 0)
    lax.fori_loop(0, 3, attend_own_row, 0)
    spread_wo(3)
    lax.fori_loop(3, 4, attend_own_row, 0)
    orx[0] = otx[0]
    strx[0] = sttx[0]
    for i in range(1, 4):
        arrived(orx.at[i], S_O + i)
        arrived(strx.at[i], S_ST + i)
    tops = [strx[i][0:1, :] for i in range(4)]
    top = functools.reduce(jnp.maximum, tops)
    total = jnp.zeros((1, 256), F32)
    weighted = jnp.zeros((HD, 256), F32)
    for i in range(4):
        factor = jnp.exp(tops[i] - top)
        total = total + factor * strx[i][1:2, :]
        weighted = weighted + orx[i].astype(F32) * factor
    mixed[0] = (weighted / total).T.astype(BF16)
    pltpu.make_async_copy(sqkv.at[b], sqkv.at[b], ls.at[6]).wait()
    self_loads[3].wait()
    spread_self(0)
    spread_wo(4)
    spread_wo(5)

    def project_and_sum(u, weight, between, finish):
        for h in range(2):
            def columns_of(i, carry):
                columns = pl.ds(pl.multiple_of(i * 512, 512), 512)
                y = dot(mixed[u], weight[i]).reshape(8, 2, 2, 8, 512)
                for cc in range(2):
                    part[u, cc, :, :, columns] = y[:, :, cc].reshape(8, 16, 512).astype(BF16)
                return carry

            lax.fori_loop(4 * h, 4 * h + 4, columns_of, 0)
            send(
                part.at[u, 1 - c, :, :, half_columns(h)], sib.at[u, :, :, half_columns(h)],
                S_RSC + 2 * u + h, sibling,
            )

        def chip_sum(zz, h):
            columns = half_columns(h)
            return part[u, c, zz, :, columns].astype(F32) + sib[u, zz, :, columns].astype(F32)

        def hop(k, way, h, start):
            if k == start and way == h:
                arrived(sib.at[u, :, :, half_columns(h)], S_RSC + 2 * u + h)
            zz = (z + k) % 8 if way == 0 else (z + 8 - k) % 8
            value = chip_sum(zz, h)
            at = S_RSZ + ((u * 2 + way) * 2 + h) * 4
            if k < start:
                arrived(rrx.at[u, way, h, k], at + k + 1)
                value = value + rrx[u, way, h, k].astype(F32)
            rtx[u, way, h, k - 1] = value.astype(BF16)
            send(rtx.at[u, way, h, k - 1], rrx.at[u, way, h, k - 1], at + k, vertical[way])

        for k in (4, 3, 2, 1):
            hop(k, 0, 0, 4)
            hop(k, 1, 1, 4)
            if k > 1:
                hop(k - 1, 0, 1, 3)
                hop(k - 1, 1, 0, 3)
            between(k)
        for h in range(2):
            value = chip_sum(z, h)
            for way in range(2):
                arrived(rrx.at[u, way, h, 0], S_RSZ + ((u * 2 + way) * 2 + h) * 4 + 1)
                value = value + rrx[u, way, h, 0].astype(F32)
            finish(h, value)

    def between_cross(k):
        if k == 3:
            spread_self(1)
        if k == 1:
            spread_self(2)

    def finish_cross(h, value):
        columns = half_columns(h)
        carried16[:, columns] = latent16[:, columns] + value
        ztx[:, columns] = value.astype(BF16)
        send(ztx.at[:, columns], zrx.at[:, columns], S_RSY + h, across)

    project_and_sum(0, wo, between_cross, finish_cross)
    for h in range(2):
        arrived(zrx.at[:, half_columns(h)], S_RSY + h)
    carried = carried16[...] + zrx[...].astype(F32)
    own_carried = jnp.where(yh == 0, carried[:8], carried[8:])

    gather_begin(1, carried, gain_s[...])
    spread_self(3)
    spread_so(0)

    def arrived_rows(places):
        return jnp.concatenate([gat[1, (z + 8 - k) % 8].reshape(32, D) for k in places], axis=0)

    def keyval(places, start):
        rows = natural(dot(arrived_rows(places), sqkv[:, :, HD:].reshape(D, 2 * HD)), 2 * HD)
        kv2[b, pl.ds(start, 32 * len(places))] = rows.astype(BF16)

    def spread_keyval(stage, parts):
        for n in parts:
            start, rows = ((0, 64), (64, 96), (160, 32), (192, 64))[n]
            spread(kv2, start, rows, S_KV2 + 7 * n, n % 2 == 1, stage)

    near, far = (0, 1, 7, 2, 6), (3, 5, 4)
    gather_step(1, 1)
    gather_step(1, 2)
    spread_so(1)
    gather_step(1, 3)
    spread_self(4)
    spread_self(5)
    gather_end(1, near)
    keyval(near, 0)
    spread_keyval(0, (0, 1))
    gather_step(1, 4)
    gather_end(1, far)
    keyval(far, 160)
    spread_keyval(0, (2, 3))
    spread_keyval(1, (0, 1))
    spread_so(2)
    queries = natural(dot(latent_rows(1), sqkv[:, :, :HD].reshape(D, HD)), HD).astype(BF16)

    def absorb(source, own):
        block = kv2[source]
        s = dot(block[:, :HD], queries, 1, 1) * SCALE
        if own:
            row = lax.broadcasted_iota(jnp.int32, (256, 256), 0)
            place = row >> 5
            distance = (place + 1) >> 1
            ids = ((z + 8 + jnp.where((place & 1) == 1, -distance, distance)) & 7) * 32 + (row & 31)
            s = jnp.where(ids <= lax.broadcasted_iota(jnp.int32, (256, 256), 1), s, LOW)
        top = jnp.max(s, axis=0, keepdims=True)
        if not own:
            top = jnp.maximum(top, top2[...])
        e = jnp.exp(s - top)
        total = jnp.sum(e, axis=0, keepdims=True)
        weighted = dot(block[:, HD:], e.astype(BF16), 0, 0)
        if not own:
            factor = jnp.exp(top2[...] - top)
            total = total + total2[...] * factor
            weighted = weighted + weighted2[...] * factor
        top2[...] = top
        total2[...] = total
        weighted2[...] = weighted

    def absorb_earlier(*slots):
        for i in slots:
            @pl.when(blk_from(i) < b)
            def _():
                absorb(blk_from(i), False)

    absorb(b, True)
    spread_keyval(2, (0, 1))
    spread_keyval(1, (2, 3))
    spread_keyval(3, (0, 1))
    spread_keyval(2, (2, 3))
    spread_so(3)
    spread_keyval(3, (2, 3))
    spread_keyval(4, range(4))
    absorb_earlier(1, 3, 2)
    spread_keyval(5, range(4))
    absorb_earlier(4, 5, 7, 6)
    mixed[1] = (weighted2[...] / total2[...]).T.astype(BF16)

    spread_so(4)
    spread_so(5)
    def finish_self(h, value):
        columns = half_columns(h)
        out[:, columns] = own_carried[:, columns.start:columns.start + HALF] + jnp.where(yh == 0, value[:8], value[8:])
        ytx[h] = pack_rows(jnp.where(yh == 0, value[8:], value[:8])).astype(BF16)
        send(ytx.at[h], yrx.at[h], S_RSY + 2 + h, across)

    project_and_sum(1, so, lambda k: None, finish_self)
    for h in range(2):
        columns = half_columns(h)
        arrived(yrx.at[h], S_RSY + 2 + h)
        out[:, columns] = out[:, columns] + unpack_rows(yrx[h].astype(F32))

    for group, kib in enumerate(sent_kib):
        everything = scores.at[pl.ds(0, kib)]
        remote(everything, everything, 0, sibling, group).wait_send()
    remote(sttx.at[pl.ds(0, 7)], strx.at[pl.ds(0, 7)], 0, sibling, N_GROUPS - 1).wait_send()


def shards(*arguments):
    prefix, latent, limits, gain_p, gain_l, gain_s, *weights = arguments
    vmem = pl.BlockSpec(memory_space=pltpu.VMEM)
    sem = pltpu.SemaphoreType.DMA
    scratch = [
        ((6, 512, HD), BF16),
        ((2, HD, 512), BF16),
        ((1024, D), BF16),
        ((8, 512, 3 * HD), BF16),
        ((8, HD, 512), BF16),
        ((8, 512, 3 * HD), BF16),
        ((8, HD, 512), BF16),
        ((8, 8, 256), jnp.int32),
        ((8, 256, HD), BF16),
        ((1280, HD), BF16),
        ((HD, 1280), BF16),
        ((1024, 2 * HD), F32),
        ((1280, 256), F32),
        ((8, HD, 256), BF16),
        ((8, HD, 256), BF16),
        ((8, 2, 256), F32),
        ((8, 2, 256), F32),
        ((2, 256, HD), BF16),
        ((8, 256, 2 * HD), BF16),
        ((1, 256), F32),
        ((1, 256), F32),
        ((HD, 256), F32),
        ((16, HALF), BF16),
        ((16, HALF), BF16),
        ((2, 8, 2, 16, D), BF16),
        ((2, 2, 8, 16, D), BF16),
        ((2, 8, 16, D), BF16),
        ((2, 2, 2, 4, 16, HALF), BF16),
        ((2, 2, 2, 4, 16, HALF), BF16),
        ((2, 16, HALF // 2), BF16),
        ((2, 16, HALF // 2), BF16),
        ((16, D), BF16),
        ((16, D), BF16),
        ((16, D), F32),
        ((16, D), F32),
    ]
    return pl.pallas_call(
        layer_kernel,
        out_shape=jax.ShapeDtypeStruct((8, D), F32),
        in_specs=[pl.BlockSpec(memory_space=pl.ANY)] + [vmem] * 5
        + [pl.BlockSpec(memory_space=pl.ANY)] * 12,
        out_specs=vmem,
        scratch_shapes=[pltpu.VMEM(shape, dtype) for shape, dtype in scratch]
        + [sem((N_GROUPS,)), sem((N_SEM,)), sem((8,))],
        compiler_params=pltpu.CompilerParams(
            collective_id=0, has_side_effects=True, vmem_limit_bytes=56 * 1024 * 1024
        ),
        name="layer",
    )(
        prefix, latent, limits.reshape(1, -1),
        gain_p.reshape(1, -1), gain_l.reshape(1, -1), gain_s.reshape(1, -1), *weights,
    )


def solution(mesh):
    return jax.shard_map(
        shards,
        mesh=mesh,
        in_specs=(
            P("blk", None), P(("blk", "grp"), None), P("blk"), P(), P(), P(),
            P("blk", "grp"), P("blk", "grp"), P("blk", "grp"), P("grp", "blk"),
            P("blk", "grp"), P("blk", "grp"), P("blk", "grp"), P("grp", "blk"),
            P("blk", "grp"), P("blk", "grp"), P("blk", "grp"), P("grp", "blk"),
        ),
        out_specs=P(("blk", "grp"), None),
        check_vma=False,
    )
```

```python
import functools
import math

import jax
import jax.numpy as jnp
from jax import lax
from jax.experimental import pallas as pl
from jax.experimental.pallas import tpu as pltpu
from jax.sharding import PartitionSpec as P

D = 4096
HD = 128
HALF = D // 2
EPS = 1e-05
SCALE = HD ** (-0.5)
LOW = -1e30
CLIP = -1e20
MESH = pl.DeviceIdType.MESH
F32 = jnp.float32
BF16 = jnp.bfloat16

N_SEM = 0


def _places(count):
    global N_SEM
    first = N_SEM
    N_SEM += count
    return first


S_W = _places(4 * 7) - 1
S_WO = _places(7) - 1
S_SQKV = _places(7) - 1
S_SO = _places(7) - 1
S_LIM = _places(1)
S_Q = _places(7) - 1
S_O = _places(7) - 1
S_ST = _places(7) - 1
S_KV2 = _places(4 * 7) - 1
S_AGY = _places(1)
S_AGZ = _places(2 * 2 * 7)
S_AGC = _places(3)
S_RSC = _places(4)
S_RSZ = _places(2 * 2 * 2 * 4) - 1
S_RSY = _places(4)

GROUP_KIB = 1100
N_GROUPS = 18


def rms_rows(values, gain):
    inverse = lax.rsqrt(jnp.sum(values * values, axis=1, keepdims=True) * (1.0 / D) + EPS)
    return values * inverse * gain


def pack_rows(rows):
    half = rows.shape[1] // 2
    return jnp.concatenate([rows[:, :half], rows[:, half:]], axis=0)


def unpack_rows(packed):
    return jnp.concatenate([packed[:8], packed[8:]], axis=1)


def dot(a, b, ca=1, cb=0):
    return lax.dot_general(a, b, (((ca,), (cb,)), ((), ())), preferred_element_type=F32)


def layer_kernel(
    prefix, latent, limits, gain_p, gain_l, gain_s,
    cq, ck, cv, co, dq, dk, dv, do, sq, sk, sv, so_in,
    out,
    raw, raw_o, pre, wqkv, wo, sqkv, so, lim, qn, kn, vt, acc, scores,
    otx, orx, sttx, strx, mixed, kv2, top2, total2, weighted2,
    pk, pkr, gat, part, sib, rtx, rrx, ytx, yrx, ztx, zrx, latent16, carried16,
    ss, rs, ls,
):
    b = lax.axis_index("blk")
    g = lax.axis_index("grp")
    x, yl = b % 4, b // 4
    z, yh, c = g // 4, (g // 2) % 2, g % 2

    def blk_to(i):
        return {"blk": ((yl + i // 4) % 2) * 4 + (x + i % 4) % 4, "grp": g}

    def blk_from(i):
        return ((yl + i // 4) % 2) * 4 + (x + 4 - i % 4) % 4

    def grp_at(zz, yy, cc):
        return {"blk": b, "grp": (zz * 2 + yy) * 2 + cc}

    sibling = grp_at(z, yh, 1 - c)
    across = grp_at(z, 1 - yh, c)
    above = grp_at((z + 1) % 8, yh, c)
    below = grp_at((z + 7) % 8, yh, c)
    vertical = (above, below)

    def remote(src, dst, place, device, group=0):
        return pltpu.make_async_remote_copy(
            src_ref=src, dst_ref=dst, send_sem=ss.at[group], recv_sem=rs.at[place],
            device_id=device, device_id_type=MESH,
        )

    sent_kib = [0]

    def group_for(src, count=1):
        kib = count * math.prod(src.shape) * jnp.dtype(src.dtype).itemsize // 1024
        if sent_kib[-1] + kib > GROUP_KIB and sent_kib[-1] % 8 == 0:
            sent_kib.append(0)
        sent_kib[-1] += kib
        return len(sent_kib) - 1

    def send(src, dst, place, device):
        remote(src, dst, place, device, group_for(src)).start()

    def arrived(dst, place):
        remote(dst, dst, place, sibling).wait_recv()

    barrier = pltpu.get_barrier_semaphore()
    for i in range(1, 8):
        pl.semaphore_signal(barrier, inc=1, device_id=blk_to(i), device_id_type=MESH)
    for device in (sibling, across, above, below):
        pl.semaphore_signal(barrier, inc=1, device_id=device, device_id_type=MESH)

    loads = [
        pltpu.make_async_copy(prefix.at[pl.ds(t * 256, 256)], pre.at[pl.ds(t * 256, 256)], ls.at[t])
        for t in range(4)
    ]
    raw_loads = [
        pltpu.make_async_copy(source, raw.at[n], ls.at[4]) for n, source in enumerate((cq, ck, cv, dq, dk, dv))
    ] + [
        pltpu.make_async_copy(source, raw_o.at[n], ls.at[5]) for n, source in enumerate((co, do))
    ]
    self_loads = [
        pltpu.make_async_copy(source, sqkv.at[b, :, pl.ds(n * HD, HD)], ls.at[6])
        for n, source in enumerate((sq, sk, sv))
    ] + [pltpu.make_async_copy(so_in, so.at[b], ls.at[7])]
    for load in raw_loads + self_loads:
        load.start()
    for load in loads:
        load.start()

    def perturbed(weight, delta):
        return (weight.astype(F32) + delta.astype(F32)).astype(BF16)

    rows_l = latent[...].astype(F32)
    pk[...] = pack_rows(rows_l).astype(BF16)
    lim[0] = jnp.broadcast_to(limits[...], (8, 256))
    pltpu.make_async_copy(raw, raw, ls.at[4]).wait()
    for n in range(3):
        wqkv[b, :, n * HD:(n + 1) * HD] = perturbed(raw[n], raw[n + 3])
    pl.semaphore_wait(barrier, 11)

    right, left, beside = blk_to(1), blk_to(3), blk_to(4)

    def spread(buf, start, rows, place, y_first, stage):
        def here(i, piece=None):
            if piece is None:
                return buf.at[blk_from(i), pl.ds(start, rows)]
            return buf.at[blk_from(i), pl.ds(start + piece * (rows // 2), rows // 2)]

        if stage == 0:
            send(here(0), here(0), place + 4, beside)
            send(here(0), here(0), place + 1, right)
            send(here(0), here(0), place + 3, left)
        elif y_first and stage == 1:
            arrived(here(4), place + 4)
            send(here(4), here(4), place + 5, right)
            send(here(4), here(4), place + 7, left)
        elif y_first and stage == 2:
            arrived(here(1), place + 1)
            send(here(1, 0), here(1, 0), place + 2, right)
            arrived(here(3), place + 3)
            send(here(3, 1), here(3, 1), place + 2, left)
        elif y_first and stage == 3:
            arrived(here(5), place + 5)
            send(here(5, 0), here(5, 0), place + 6, right)
            arrived(here(7), place + 7)
            send(here(7, 1), here(7, 1), place + 6, left)
        elif y_first and stage == 4:
            arrived(here(2), place + 2)
        elif y_first:
            arrived(here(6), place + 6)
        elif stage == 1:
            arrived(here(1), place + 1)
            send(here(1, 0), here(1, 0), place + 2, right)
            send(here(1), here(1), place + 5, beside)
            arrived(here(3), place + 3)
            send(here(3, 1), here(3, 1), place + 2, left)
            send(here(3), here(3), place + 7, beside)
        elif stage == 2:
            arrived(here(2), place + 2)
            send(here(2), here(2), place + 6, beside)
        elif stage == 5:
            for i in (4, 5, 7, 6):
                arrived(here(i), place + i)

    def spread_cross(stage, parts):
        for n in parts:
            start, rows = ((0, 96), (96, 160), (256, 128), (384, 128))[n]
            spread(wqkv, start, rows, S_W + 7 * n, n % 2 == 1, stage)

    def spread_self(stage):
        spread(sqkv, 0, 512, S_SQKV, True, stage)

    def spread_wo(stage):
        spread(wo, 0, HD, S_WO, True, stage)

    def spread_so(stage):
        spread(so, 0, HD, S_SO, True, stage)

    def own_and_other(own, other):
        return jnp.concatenate([jnp.where(yh == 0, own, other), jnp.where(yh == 0, other, own)], axis=0)

    def half_columns(h):
        return pl.ds(h * HALF, HALF)

    def agz(u, way, k, h):
        return S_AGZ + (u * 2 + way) * 7 + (k - 1) * 2 + (h if k < 4 else 0)

    def agc(u, place):
        return S_AGC + (u if place not in (3, 4, 5) else 2 * u)

    def gather_begin(u, rows, gain):
        gat[u, z, c] = rms_rows(rows, gain).astype(BF16)
        for n in range(2):
            for way in range(2):
                h = n if way == 0 else 1 - n
                own = gat.at[u, z, c, :, half_columns(h)]
                send(own, own, agz(u, way, 1, h), vertical[way])
        for h in range(2):
            own = gat.at[u, z, c, :, half_columns(h)]
            send(own, own, agc(u, 0), sibling)

    def gather_step(u, k):
        for n in range(2):
            for way in range(2):
                h = n if way == 0 else 1 - n
                if k == 4 and n == 1:
                    continue
                zz = (z + 8 - k) % 8 if way == 0 else (z + k) % 8
                chunk = gat.at[u, zz, c, :, half_columns(h)]
                arrived(chunk, agz(u, way, k, h))
                if k < 3 or k == 3 and n == 0:
                    send(chunk, chunk, agz(u, way, k + 1, h), vertical[way])
                send(chunk, chunk, agc(u, k if way == 0 else 8 - k), sibling)

    def gather_end(u, places):
        arrived(gat.at[u, pl.ds(0, len(places)), 1 - c], agc(u, places[0]))

    send(pk, pkr, S_AGY, across)
    spread_cross(0, (0, 1, 2, 3))
    for i in range(1, 8):
        send(lim.at[0], lim.at[i], S_LIM, blk_to(i))

    def norm_prefix(t):
        if t % 2 == 0:
            loads[t // 2].wait()

        def tile(n, carry):
            rows = pl.ds(pl.multiple_of(t * 128 + n * 16, 16), 16)
            pre[rows, :] = rms_rows(pre[rows, :].astype(F32), gain_p[...]).astype(BF16)
            return carry

        lax.fori_loop(0, 8, tile, 0)

    def prefix_part(row, first):
        columns = pl.ds(pl.multiple_of(row * HALF, HALF), HALF)
        weights = wqkv[pl.ds(row * 4, 4), :, HD:].reshape(HALF, 2 * HD)
        for t in range(2):
            rows = pl.ds(t * 512, 512)
            piece = dot(pre[rows, columns], weights)
            acc[rows, :] = piece if first else acc[rows, :] + piece

    def latent_rows(u):
        return gat[u].reshape(256, D)

    def natural(values, width):
        cut = values.reshape(-1, 2, 2, 8, width)
        order = jnp.stack([cut[:, cc, yy] for yy in range(2) for cc in range(2)], axis=1)
        return order.reshape(values.shape[0], width)

    norm_prefix(0)
    arrived(pkr, S_AGY)
    latent16[...] = own_and_other(rows_l, unpack_rows(pkr[...].astype(F32)))
    gather_begin(0, latent16[...], gain_l[...])
    norm_prefix(1)
    spread_cross(1, (0, 1))
    gather_step(0, 1)
    norm_prefix(2)
    gather_step(0, 2)
    spread_cross(1, (2, 3))
    norm_prefix(3)
    spread_cross(2, (0, 1))
    norm_prefix(4)
    gather_step(0, 3)
    spread_cross(2, (2, 3))
    norm_prefix(5)
    spread_cross(3, (0, 1))
    gather_step(0, 4)
    norm_prefix(6)
    spread_cross(3, (2, 3))
    pltpu.make_async_copy(raw_o, raw_o, ls.at[5]).wait()
    wo[b] = perturbed(raw_o[0], raw_o[1])
    spread_wo(0)
    norm_prefix(7)
    spread_cross(4, (0, 1, 2, 3))
    prefix_part(yl, True)
    gather_end(0, range(8))
    spread_cross(5, (0, 1, 2, 3))
    qn[0] = natural(dot(latent_rows(0), wqkv[:, :, :HD].reshape(D, HD)), HD).astype(BF16)
    for i in (4, 5, 7, 6, 1, 3, 2):
        send(qn.at[0], qn.at[i], S_Q + i, blk_to(i))
    prefix_part(1 - yl, False)
    spread_wo(1)
    latent_kv = natural(dot(latent_rows(0), wqkv[:, :, HD:].reshape(D, 2 * HD)), 2 * HD)
    for t in range(5):
        rows = pl.ds(t * 256, 256)
        values = acc[rows, :] if t < 4 else latent_kv
        kn[rows, :] = values[:, :HD].astype(BF16)
        vt[:, rows] = values[:, HD:].T.astype(BF16)

    def attend(i):
        source = blk_from(i)
        queries = qn[i]
        seen = lim[i][0:1, :]
        high = jnp.full((8, 256), CLIP, F32)
        for t in range(5):
            s = dot(kn[pl.ds(t * 256, 256), :], queries, 1, 1) * SCALE
            ids = lax.broadcasted_iota(jnp.int32, (256, 256), 0)
            if t < 4:
                allowed = ids + (b * 1024 + t * 256) < seen
            else:
                allowed = ids + b * 256 <= lax.broadcasted_iota(jnp.int32, (256, 256), 1) + source * 256
            s = jnp.where(allowed, s, LOW)
            scores[pl.ds(t * 256, 256), :] = s
            high = jnp.maximum(high, jnp.max(s.reshape(32, 8, 256), axis=0))
        top = jnp.max(high, axis=0, keepdims=True)
        total = jnp.zeros((8, 256), F32)
        weighted = jnp.zeros((HD, 256), F32)
        for t in range(5):
            e = jnp.exp(scores[pl.ds(t * 256, 256), :] - top)
            total = total + jnp.sum(e.reshape(32, 8, 256), axis=0)
            weighted = weighted + dot(vt[:, pl.ds(t * 256, 256)], e.astype(BF16))
        return top, jnp.sum(total, axis=0, keepdims=True), weighted

    def keep(i, top, total, weighted):
        otx[i] = weighted.astype(BF16)
        first = lax.broadcasted_iota(jnp.int32, (2, 256), 0) == 0
        sttx[i] = jnp.where(first, top, total)

    output_group = group_for(otx.at[0], 7)

    def across_copies(i):
        return (
            remote(otx.at[i], orx.at[i], S_O + i, beside, output_group),
            remote(sttx.at[i], strx.at[i], S_ST + i, beside, N_GROUPS - 1),
        )

    def along_copies(i):
        back = {"blk": blk_from(i), "grp": g}
        return (
            remote(otx.at[i], orx.at[i], S_O + i, back, output_group),
            remote(sttx.at[i], strx.at[i], S_ST + i, back, N_GROUPS - 1),
        )

    def attend_partner_row(n, carry):
        i = n + 4
        arrived(qn.at[i], S_Q + i)
        keep(i, *attend(i))
        for copy in across_copies(i):
            copy.start()
        return carry

    def attend_own_row(n, carry):
        i = (n + 1) % 4

        @pl.when(i > 0)
        def _():
            arrived(qn.at[i], S_Q + i)

        top, total, weighted = attend(i)
        arrived(orx.at[i + 4], S_O + i + 4)
        arrived(strx.at[i + 4], S_ST + i + 4)
        top_there = strx[i + 4][0:1, :]
        both = jnp.maximum(top, top_there)
        here_part, there_part = jnp.exp(top - both), jnp.exp(top_there - both)
        keep(
            i, both, total * here_part + strx[i + 4][1:2, :] * there_part,
            weighted * here_part + orx[i + 4].astype(F32) * there_part,
        )

        @pl.when(i > 0)
        def _():
            for copy in along_copies(i):
                copy.start()

        return carry

    spread_wo(2)
    arrived(lim.at[pl.ds(1, 7)], S_LIM)
    lax.fori_loop(0, 4, attend_partner_row, 0)
    lax.fori_loop(0, 1, attend_own_row, 0)
    spread_wo(3)
    lax.fori_loop(1, 4, attend_own_row, 0)
    orx[0] = otx[0]
    strx[0] = sttx[0]
    for i in range(1, 4):
        arrived(orx.at[i], S_O + i)
        arrived(strx.at[i], S_ST + i)
    tops = [strx[i][0:1, :] for i in range(4)]
    top = functools.reduce(jnp.maximum, tops)
    total = jnp.zeros((1, 256), F32)
    weighted = jnp.zeros((HD, 256), F32)
    for i in range(4):
        factor = jnp.exp(tops[i] - top)
        total = total + factor * strx[i][1:2, :]
        weighted = weighted + orx[i].astype(F32) * factor
    mixed[0] = (weighted / total).T.astype(BF16)
    pltpu.make_async_copy(sqkv.at[b], sqkv.at[b], ls.at[6]).wait()
    self_loads[3].wait()
    spread_self(0)
    spread_wo(4)
    spread_wo(5)

    def project_and_sum(u, weight, between, finish):
        for h in range(2):
            def columns_of(i, carry):
                columns = pl.ds(pl.multiple_of(i * 512, 512), 512)
                y = dot(mixed[u], weight[i]).reshape(8, 2, 2, 8, 512)
                for cc in range(2):
                    part[u, cc, :, :, columns] = y[:, :, cc].reshape(8, 16, 512).astype(BF16)
                return carry

            lax.fori_loop(4 * h, 4 * h + 4, columns_of, 0)
            send(
                part.at[u, 1 - c, :, :, half_columns(h)], sib.at[u, :, :, half_columns(h)],
                S_RSC + 2 * u + h, sibling,
            )

        def chip_sum(zz, h):
            columns = half_columns(h)
            return part[u, c, zz, :, columns].astype(F32) + sib[u, zz, :, columns].astype(F32)

        def hop(k, way, h, start):
            if k == start and way == h:
                arrived(sib.at[u, :, :, half_columns(h)], S_RSC + 2 * u + h)
            zz = (z + k) % 8 if way == 0 else (z + 8 - k) % 8
            value = chip_sum(zz, h)
            at = S_RSZ + ((u * 2 + way) * 2 + h) * 4
            if k < start:
                arrived(rrx.at[u, way, h, k], at + k + 1)
                value = value + rrx[u, way, h, k].astype(F32)
            rtx[u, way, h, k - 1] = value.astype(BF16)
            send(rtx.at[u, way, h, k - 1], rrx.at[u, way, h, k - 1], at + k, vertical[way])

        for k in (4, 3, 2, 1):
            hop(k, 0, 0, 4)
            hop(k, 1, 1, 4)
            if k > 1:
                hop(k - 1, 0, 1, 3)
                hop(k - 1, 1, 0, 3)
            between(k)
        for h in range(2):
            value = chip_sum(z, h)
            for way in range(2):
                arrived(rrx.at[u, way, h, 0], S_RSZ + ((u * 2 + way) * 2 + h) * 4 + 1)
                value = value + rrx[u, way, h, 0].astype(F32)
            finish(h, value)

    def between_cross(k):
        if k == 3:
            spread_self(1)
        if k == 1:
            spread_self(2)

    def finish_cross(h, value):
        columns = half_columns(h)
        carried16[:, columns] = latent16[:, columns] + value
        ztx[:, columns] = value.astype(BF16)
        send(ztx.at[:, columns], zrx.at[:, columns], S_RSY + h, across)

    project_and_sum(0, wo, between_cross, finish_cross)
    for h in range(2):
        arrived(zrx.at[:, half_columns(h)], S_RSY + h)
    carried = carried16[...] + zrx[...].astype(F32)
    own_carried = jnp.where(yh == 0, carried[:8], carried[8:])

    gather_begin(1, carried, gain_s[...])
    spread_self(3)
    spread_so(0)

    def arrived_rows(places):
        return jnp.concatenate([gat[1, (z + 8 - k) % 8].reshape(32, D) for k in places], axis=0)

    def keyval(places, start):
        rows = natural(dot(arrived_rows(places), sqkv[:, :, HD:].reshape(D, 2 * HD)), 2 * HD)
        kv2[b, pl.ds(start, 32 * len(places))] = rows.astype(BF16)

    def spread_keyval(stage, parts):
        for n in parts:
            start, rows = ((0, 64), (64, 96), (160, 32), (192, 64))[n]
            spread(kv2, start, rows, S_KV2 + 7 * n, n % 2 == 1, stage)

    near, far = (0, 1, 7, 2, 6), (3, 5, 4)
    gather_step(1, 1)
    spread_so(1)
    gather_step(1, 2)
    spread_so(2)
    gather_step(1, 3)
    spread_self(4)
    spread_self(5)
    spread_so(3)
    gather_end(1, near)
    keyval(near, 0)
    spread_keyval(0, (0, 1))
    gather_step(1, 4)
    gather_end(1, far)
    keyval(far, 160)
    spread_keyval(0, (2, 3))
    spread_keyval(1, (0, 1))
    queries = natural(dot(latent_rows(1), sqkv[:, :, :HD].reshape(D, HD)), HD).astype(BF16)

    def absorb(source, own):
        block = kv2[source]
        s = dot(block[:, :HD], queries, 1, 1) * SCALE
        if own:
            row = lax.broadcasted_iota(jnp.int32, (256, 256), 0)
            place = row >> 5
            distance = (place + 1) >> 1
            ids = ((z + 8 + jnp.where((place & 1) == 1, -distance, distance)) & 7) * 32 + (row & 31)
            s = jnp.where(ids <= lax.broadcasted_iota(jnp.int32, (256, 256), 1), s, LOW)
        top = jnp.max(s, axis=0, keepdims=True)
        if not own:
            top = jnp.maximum(top, top2[...])
        e = jnp.exp(s - top)
        total = jnp.sum(e, axis=0, keepdims=True)
        weighted = dot(block[:, HD:], e.astype(BF16), 0, 0)
        if not own:
            factor = jnp.exp(top2[...] - top)
            total = total + total2[...] * factor
            weighted = weighted + weighted2[...] * factor
        top2[...] = top
        total2[...] = total
        weighted2[...] = weighted

    def absorb_earlier(*slots):
        for i in slots:
            @pl.when(blk_from(i) < b)
            def _():
                absorb(blk_from(i), False)

    absorb(b, True)
    spread_keyval(2, (0, 1))
    spread_keyval(1, (2, 3))
    spread_keyval(3, (0, 1))
    spread_keyval(2, (2, 3))
    spread_keyval(3, (2, 3))
    spread_keyval(4, range(4))
    absorb_earlier(1, 3, 2)
    spread_keyval(5, range(4))
    absorb_earlier(4, 5, 7, 6)
    mixed[1] = (weighted2[...] / total2[...]).T.astype(BF16)

    spread_so(4)
    spread_so(5)
    def finish_self(h, value):
        columns = half_columns(h)
        out[:, columns] = own_carried[:, columns.start:columns.start + HALF] + jnp.where(yh == 0, value[:8], value[8:])
        ytx[h] = pack_rows(jnp.where(yh == 0, value[8:], value[:8])).astype(BF16)
        send(ytx.at[h], yrx.at[h], S_RSY + 2 + h, across)

    project_and_sum(1, so, lambda k: None, finish_self)
    for h in range(2):
        columns = half_columns(h)
        arrived(yrx.at[h], S_RSY + 2 + h)
        out[:, columns] = out[:, columns] + unpack_rows(yrx[h].astype(F32))

    for group, kib in enumerate(sent_kib):
        everything = scores.at[pl.ds(0, kib)]
        remote(everything, everything, 0, sibling, group).wait_send()
    remote(sttx.at[pl.ds(0, 7)], strx.at[pl.ds(0, 7)], 0, sibling, N_GROUPS - 1).wait_send()


def shards(*arguments):
    prefix, latent, limits, gain_p, gain_l, gain_s, *weights = arguments
    vmem = pl.BlockSpec(memory_space=pltpu.VMEM)
    sem = pltpu.SemaphoreType.DMA
    scratch = [
        ((6, 512, HD), BF16),
        ((2, HD, 512), BF16),
        ((1024, D), BF16),
        ((8, 512, 3 * HD), BF16),
        ((8, HD, 512), BF16),
        ((8, 512, 3 * HD), BF16),
        ((8, HD, 512), BF16),
        ((8, 8, 256), jnp.int32),
        ((8, 256, HD), BF16),
        ((1280, HD), BF16),
        ((HD, 1280), BF16),
        ((1024, 2 * HD), F32),
        ((1280, 256), F32),
        ((8, HD, 256), BF16),
        ((8, HD, 256), BF16),
        ((8, 2, 256), F32),
        ((8, 2, 256), F32),
        ((2, 256, HD), BF16),
        ((8, 256, 2 * HD), BF16),
        ((1, 256), F32),
        ((1, 256), F32),
        ((HD, 256), F32),
        ((16, HALF), BF16),
        ((16, HALF), BF16),
        ((2, 8, 2, 16, D), BF16),
        ((2, 2, 8, 16, D), BF16),
        ((2, 8, 16, D), BF16),
        ((2, 2, 2, 4, 16, HALF), BF16),
        ((2, 2, 2, 4, 16, HALF), BF16),
        ((2, 16, HALF // 2), BF16),
        ((2, 16, HALF // 2), BF16),
        ((16, D), BF16),
        ((16, D), BF16),
        ((16, D), F32),
        ((16, D), F32),
    ]
    return pl.pallas_call(
        layer_kernel,
        out_shape=jax.ShapeDtypeStruct((8, D), F32),
        in_specs=[pl.BlockSpec(memory_space=pl.ANY)] + [vmem] * 5
        + [pl.BlockSpec(memory_space=pl.ANY)] * 12,
        out_specs=vmem,
        scratch_shapes=[pltpu.VMEM(shape, dtype) for shape, dtype in scratch]
        + [sem((N_GROUPS,)), sem((N_SEM,)), sem((8,))],
        compiler_params=pltpu.CompilerParams(
            collective_id=0, has_side_effects=True, vmem_limit_bytes=56 * 1024 * 1024
        ),
        name="layer",
    )(
        prefix, latent, limits.reshape(1, -1),
        gain_p.reshape(1, -1), gain_l.reshape(1, -1), gain_s.reshape(1, -1), *weights,
    )


def solution(mesh):
    return jax.shard_map(
        shards,
        mesh=mesh,
        in_specs=(
            P("blk", None), P(("blk", "grp"), None), P("blk"), P(), P(), P(),
            P("blk", "grp"), P("blk", "grp"), P("blk", "grp"), P("grp", "blk"),
            P("blk", "grp"), P("blk", "grp"), P("blk", "grp"), P("grp", "blk"),
            P("blk", "grp"), P("blk", "grp"), P("blk", "grp"), P("grp", "blk"),
        ),
        out_specs=P(("blk", "grp"), None),
        check_vma=False,
    )
```
